512 devices in a mesh: qb: 16 (over y_lo, z), kb: 16 (over y_hi, x), pair: 2 (over core).
Axes of the slice: x: 4, y: 8 (y_hi: 4, y_lo: 2; y = y_hi * 2 + y_lo), z: 8, core: 2. Of those that a mesh axis runs over, the one named last changes fastest.
Arguments:
- queries: bfloat16 [2, 32768, 256], P('pair', ('qb', 'kb')), may hold values from -24 to 24
- keys: bfloat16 [2, 32768, 256], P('pair', ('kb', 'qb')), may hold values from -24 to 24
- values: bfloat16 [2, 32768, 256], P('pair', ('kb', 'qb')), may hold values from -6 to 6
- out_grad: bfloat16 [2, 32768, 256], P('pair', ('qb', 'kb')), may hold values from -0.796875 to 0.796875
- token_error: float32 [2, 32768], P('pair', ('qb', 'kb')), may hold values from 0.25 to 16
- block_mask: int32 [2, 256, 256], P(None, 'qb', 'kb'), may hold values from 0 to 1, as said below
Outputs:
- query_grad: bfloat16 [2, 32768, 256], P('pair', ('qb', 'kb'))
- key_grad: bfloat16 [2, 32768, 256], P('pair', ('kb', 'qb'))
- value_grad: bfloat16 [2, 32768, 256], P('pair', ('kb', 'qb'))
The draws below stay inside these ranges and needn't reach their ends.
Inputs may be any that keep to these rules, and one draw needn't show every extreme that they name: `block_mask`: entries are 0 or 1. With blocks in groups of 16 consecutive blocks, for every head the tile of query group a and key group b holds exactly 32 >> bitlen(|a - b|) ones, where bitlen(0) = 0, bitlen(1) = 1, bitlen(2) = bitlen(3) = 2, bitlen(4) to bitlen(7) = 3 and so on; every diagonal block (i, i) is one.
All inputs are finite; a program needn't handle non-finite values.
Results may differ from the reference program's by a relative error of at most 0.015.
Values may be sent and summed in bfloat16 or wider, within the bound.
No kernel may reach another device: no remote copies, remote signals or barrier semaphores. Data moves between devices by JAX's collectives and lax.ppermute only.
A program may use at most 64 MiB of HBM per device.

```python
import jax
import jax.numpy as jnp
from jax import lax

DH = 128
HEADS = 2
BLK = 128
TOKENS = 32768
NB = 256
GB = 16
CAP = 32


def drawn_rows(key):
    level = jax.random.uniform(jax.random.fold_in(key, 1), (2, TOKENS, 1), jnp.float32, 120.0, 280.0)
    strength = jnp.sqrt(level / jnp.sqrt(jnp.float32(DH)))
    pointing = jnp.clip(jax.random.normal(jax.random.fold_in(key, 2), (2, TOKENS, HEADS * DH), jnp.float32), -2.5, 2.5)
    position = jnp.arange(TOKENS) % 512
    return (strength * pointing, position)


def draw_queries(key, part):
    pattern, position = drawn_rows(key)
    key = jax.random.fold_in(key, 21)
    drawn = jnp.clip(jax.random.normal(key, (2, TOKENS, HEADS * DH), jnp.float32), -6.0, 6.0)
    drawn = jnp.where((position == 3)[None, :, None], pattern, drawn)
    return drawn.astype(jnp.bfloat16)


def draw_keys(key, part):
    pattern, position = drawn_rows(key)
    key = jax.random.fold_in(key, 22)
    drawn = jnp.clip(jax.random.normal(key, (2, TOKENS, HEADS * DH), jnp.float32), -6.0, 6.0)
    shifted = jnp.roll(pattern, 1, axis=1) * 0.99
    drawn = jnp.where((position == 3)[None, :, None], pattern, drawn)
    drawn = jnp.where((position == 4)[None, :, None], shifted, drawn)
    return drawn.astype(jnp.bfloat16)


def draw_token_error(key, part):
    key = jax.random.fold_in(key, 31)
    ramp = 1.0 + 2.0 * jnp.arange(TOKENS, dtype=jnp.float32) / TOKENS
    base = jax.random.uniform(key, (2, TOKENS), jnp.float32, 0.5, 1.5) * ramp
    return base


def draw_block_mask(key, part):
    key = jax.random.fold_in(key, 11)
    groups = NB // GB
    tile_cells = GB * GB
    random_score = jax.random.randint(key, (HEADS, groups, groups, tile_cells), 0, 1 << 16)
    cell_at = jnp.arange(tile_cells, dtype=jnp.int32)
    group_at = jnp.arange(groups, dtype=jnp.int32)
    on_diagonal = cell_at // GB == cell_at % GB
    same_group = group_at[:, None] == group_at[None, :]
    forced = same_group[:, :, None] & on_diagonal[None, None, :]
    ranked = jnp.where(forced[None], cell_at - tile_cells, random_score * tile_cells + cell_at)
    ordering = jnp.argsort(ranked, axis=-1)
    ranking = jnp.argsort(ordering, axis=-1)
    distance = jnp.abs(group_at[:, None] - group_at[None, :])
    bit_count = jnp.zeros_like(distance)
    for bit_level in range(groups.bit_length()):
        bit_count = bit_count + (distance >= 1 << bit_level).astype(jnp.int32)
    tile_total = jnp.right_shift(jnp.full_like(bit_count, CAP), bit_count)
    chosen = (ranking < tile_total[None, :, :, None]).astype(jnp.int32)
    chosen = chosen.reshape(HEADS, groups, groups, GB, GB).transpose(0, 1, 3, 2, 4)
    return chosen.reshape(HEADS, NB, NB)


def levels(stream_key, extent, pieces, low, largest):
    gain, own = 1.0, jax.random.fold_in(stream_key, 6)
    for dim, blocks in pieces:
        draws = jnp.exp(jax.random.uniform(jax.random.fold_in(own, dim), (blocks,), jnp.float32, low / len(pieces), largest / len(pieces)))
        gain = gain * jnp.repeat(draws, extent[dim] // blocks).reshape([-1 if axis == dim else 1 for axis in range(len(extent))])
    return gain


def gaussian(stream_key, shape, spread, limit, shards=(), held_as=jnp.bfloat16):
    array = spread * jax.random.normal(stream_key, shape, jnp.float32)
    if shards:
        array = array * levels(stream_key, shape, shards, -0.22, 0.18)
    return jnp.clip(array, -limit, limit).astype(held_as)


def setup_inputs(seed: int = 0) -> dict:
    seeds = jax.random.split(jax.random.key(seed), 7)
    return {
        "queries": draw_queries(jax.random.fold_in(seeds[6], 71), 0),
        "keys": draw_keys(jax.random.fold_in(seeds[6], 71), 0),
        "values": gaussian(seeds[2], (2, TOKENS, HEADS * DH), 1.0, 6.0, ((0, 2), (1, 256))),
        "out_grad": gaussian(seeds[3], (2, TOKENS, HEADS * DH), 0.1, 0.796875, ((0, 2), (1, 256))),
        "token_error": draw_token_error(jax.random.fold_in(seeds[6], 71), 0),
        "block_mask": draw_block_mask(jax.random.fold_in(seeds[6], 71), 0),
    }


beta_pref = 20.0
neg_big = -1.0e30


def rounded(value):
    return lax.optimization_barrier(value.astype(jnp.bfloat16)).astype(jnp.float32)


def tile_ones(distance):
    return CAP >> distance.bit_length()


def head_grads(query_blocks, key_blocks, value_blocks, grad_blocks, head_mask, factor):
    groups = NB // GB
    most = max(sum(tile_ones(abs(row_group - col_group)) for col_group in range(groups)) for row_group in range(groups))
    score_scale = DH ** -0.5

    def group_step(carry, row_group):
        key_acc, value_acc = carry
        base_block = (row_group * GB).astype(jnp.int32)
        rows_mask = lax.dynamic_slice_in_dim(head_mask, base_block, GB, 0)
        rows_at, cols_at = jnp.nonzero(rows_mask, size=most, fill_value=0)
        rows_at = rows_at.astype(jnp.int32)
        cols_at = cols_at.astype(jnp.int32)
        live_pair = jnp.arange(most) < jnp.sum(rows_mask)
        query_pairs = query_blocks[rows_at + base_block]
        grad_pairs = grad_blocks[rows_at + base_block]
        key_pairs = key_blocks[cols_at]
        value_pairs = value_blocks[cols_at]
        scores = jnp.einsum("pid,pjd->pij", query_pairs, key_pairs) * score_scale
        scores = jnp.where(live_pair[:, None, None], scores, neg_big)
        row_max = jnp.full((GB, BLK), neg_big, jnp.float32).at[rows_at].max(jnp.max(scores, axis=2))
        shifted = jnp.where(live_pair[:, None, None], jnp.exp(scores - row_max[rows_at][:, :, None]), 0.0)
        row_total = jnp.zeros((GB, BLK), jnp.float32).at[rows_at].add(jnp.sum(shifted, axis=2))
        weights = shifted / row_total[rows_at][:, :, None]
        grad_scores = jnp.einsum("pid,pjd->pij", grad_pairs, value_pairs)
        delta = jnp.zeros((GB, BLK), jnp.float32).at[rows_at].add(jnp.sum(weights * grad_scores, axis=2))
        dscore = rounded(weights * (grad_scores - delta[rows_at][:, :, None]))
        weights_low = rounded(weights)
        query_terms = jnp.einsum("pij,pjd->pid", dscore, key_pairs) * (score_scale * factor)
        key_terms = jnp.einsum("pij,pid->pjd", dscore, query_pairs) * (score_scale * factor)
        value_terms = jnp.einsum("pij,pid->pjd", weights_low, grad_pairs) * factor
        col_group = cols_at // GB
        query_part = jnp.zeros((GB, groups, BLK, DH), jnp.float32).at[rows_at, col_group].add(query_terms)
        query_rows = jnp.sum(rounded(query_part), axis=1).astype(jnp.bfloat16)
        key_part = jnp.zeros((NB, BLK, DH), jnp.float32).at[cols_at].add(key_terms)
        value_part = jnp.zeros((NB, BLK, DH), jnp.float32).at[cols_at].add(value_terms)
        return (key_acc + rounded(key_part), value_acc + rounded(value_part)), query_rows

    start = (jnp.zeros((NB, BLK, DH), jnp.float32), jnp.zeros((NB, BLK, DH), jnp.float32))
    (key_acc, value_acc), query_rows = lax.scan(group_step, start, jnp.arange(groups, dtype=jnp.int32))
    query_out = query_rows.reshape(TOKENS, DH)
    key_out = key_acc.reshape(TOKENS, DH).astype(jnp.bfloat16)
    value_out = value_acc.reshape(TOKENS, DH).astype(jnp.bfloat16)
    return query_out, key_out, value_out


def reference(queries, keys, values, out_grad, token_error, block_mask):
    means = jnp.sum(token_error, axis=1) / TOKENS
    keep_share = jax.nn.sigmoid(-beta_pref * (means[1] - means[0]))
    factors = (1.0 + beta_pref * keep_share, -beta_pref * keep_share)
    query_all = []
    key_all = []
    value_all = []
    for latent in range(2):
        query_heads = []
        key_heads = []
        value_heads = []
        for head_at in range(HEADS):
            def blocks_of(source):
                return source[latent].reshape(NB, BLK, HEADS, DH)[:, :, head_at, :].astype(jnp.float32)
            outs_head = head_grads(blocks_of(queries), blocks_of(keys), blocks_of(values), blocks_of(out_grad), block_mask[head_at], factors[latent])
            query_heads.append(outs_head[0])
            key_heads.append(outs_head[1])
            value_heads.append(outs_head[2])
        query_all.append(jnp.stack(query_heads, axis=1).reshape(TOKENS, HEADS * DH))
        key_all.append(jnp.stack(key_heads, axis=1).reshape(TOKENS, HEADS * DH))
        value_all.append(jnp.stack(value_heads, axis=1).reshape(TOKENS, HEADS * DH))
    return jnp.stack(query_all), jnp.stack(key_all), jnp.stack(value_all)
```

```python
import functools

import jax
import jax.numpy as jnp
from jax import lax
from jax.experimental import pallas as pl
from jax.experimental.pallas import tpu as pltpu
from jax.sharding import PartitionSpec as P

DH = 128
HEADS = 2
BLK = 128
GB = 16
WIDE = HEADS * DH
ROWS = BLK + 8
SLOTS = HEADS * GB
STAT = 3 * SLOTS + 8
LIST = 40

beta_pref = 20.0
neg_big = -1e30
score_scale = DH ** (-0.5)
log2_scale = score_scale * 1.4426950408889634

Y_GROUPS = [[x + 4 * y for y in range(4)] for x in range(4)]
X_GROUPS = [[x + 4 * y for x in range(4)] for y in range(4)]
Z_GROUPS = [[z + 8 * y for z in range(8)] for y in range(2)]
Y_PAIRS = [(s, s ^ 8) for s in range(16)]

VMEM = pl.BlockSpec(memory_space=pltpu.VMEM)
SMEM = pl.BlockSpec(memory_space=pltpu.SMEM)
ANY = pl.BlockSpec(memory_space=pl.ANY)
PARAMS = pltpu.CompilerParams(vmem_limit_bytes=40 * 1024 * 1024)


def dot(a, b, dims):
    return lax.dot_general(a, b, (dims, ((), ())), preferred_element_type=jnp.float32)


def pack_kernel(queries, keys, values, out_grad, token_error, qg_ref, kv_ref):
    qg_ref[:, :WIDE] = queries[0]
    qg_ref[:, WIDE:] = out_grad[0]
    total = jnp.sum(token_error[...], axis=1, keepdims=True)
    high = total.astype(jnp.bfloat16).astype(jnp.float32)
    rest = total - high
    middle = rest.astype(jnp.bfloat16).astype(jnp.float32)
    low = rest - middle
    row = lax.broadcasted_iota(jnp.int32, (8, 2 * WIDE), 0)
    sums = jnp.where(row == 0, high, jnp.where(row == 1, middle, jnp.where(row == 2, low, 0.0)))
    sums = jnp.concatenate([sums, jnp.zeros_like(sums)], axis=0).astype(jnp.bfloat16)[:8]
    for slot in range(8):
        kv_ref[slot, :BLK, :WIDE] = keys[0]
        kv_ref[slot, :BLK, WIDE:] = values[0]
        kv_ref[slot, BLK:, :] = sums


def list_kernel(mask, side, lists):
    for head in range(HEADS):

        def step(at, count):
            row = at // GB
            col = at % GB
            lists[2 * head, count] = (row % 4) * 4 + row // 4
            lists[2 * head + 1, count] = col ^ (side[0] * 8)
            return jnp.minimum(count + mask[head, row, col], LIST - 1)

        count = lax.fori_loop(0, GB * GB, step, 0, unroll=4)
        lists[2 * HEADS, head] = count


def load_keys(near, far, kv, sems):
    one = pltpu.make_async_copy(near, kv.at[pl.ds(0, 8)], sems.at[0])
    two = pltpu.make_async_copy(far, kv.at[pl.ds(8, 8)], sems.at[1])
    one.start()
    two.start()
    one.wait()
    two.wait()


def pair_of(lists, head, at, qg, kv):
    row, col = lists[2 * head, at], lists[2 * head + 1, at]
    first, second = head * DH, WIDE + head * DH
    query, grad = qg[row, :, first : first + DH], qg[row, :, second : second + DH]
    key, value = kv[col, :BLK, first : first + DH], kv[col, :BLK, second : second + DH]
    scores = dot(key, query, ((1,), (1,))) * log2_scale
    grad_scores = dot(value, grad, ((1,), (1,)))
    return row, col, query, grad, key, scores, grad_scores


def stat_kernel(lists, qg, near, far, stat, kv, top, total, delta, sems):
    load_keys(near, far, kv, sems)
    top[...] = jnp.full_like(top, neg_big)
    total[...] = jnp.zeros_like(total)
    delta[...] = jnp.zeros_like(delta)

    def step(p, carry):
        found = []
        for head in range(HEADS):
            for u in range(2):
                row, _, _, _, _, scores, grad_scores = pair_of(lists, head, 2 * p + u, qg, kv)
                own_top = jnp.max(scores, axis=0, keepdims=True)
                shifted = jnp.exp2(scores - own_top)
                own_total = jnp.sum(shifted, axis=0, keepdims=True)
                own_delta = jnp.sum(shifted * grad_scores, axis=0, keepdims=True)
                found.append((head * GB + row, own_top, own_total, own_delta))
        for at, own_top, own_total, own_delta in found:
            old_top = top[at]
            new_top = jnp.maximum(old_top, own_top)
            old_weight = jnp.exp2(old_top - new_top)
            own_weight = jnp.exp2(own_top - new_top)
            top[at] = new_top
            total[at] = total[at] * old_weight + own_total * own_weight
            delta[at] = delta[at] * old_weight + own_delta * own_weight
        return carry

    lax.fori_loop(0, lists[2 * HEADS, 0] // 2, step, 0)
    for at in range(SLOTS):
        stat[at : at + 1, :] = top[at]
        stat[SLOTS + at : SLOTS + at + 1, :] = total[at]
        stat[2 * SLOTS + at : 2 * SLOTS + at + 1, :] = delta[at]
    sums = kv[0, BLK:, :DH].astype(jnp.float32)
    for slot in range(1, GB):
        sums = sums + kv[slot, BLK:, :DH].astype(jnp.float32)
    sums = jnp.sum(sums, axis=0, keepdims=True)
    stat[3 * SLOTS :, :] = jnp.broadcast_to(sums, (8, DH))


def grad_kernel(lists, qg, near, far, stats, qout, kvnear, kvfar, latent, kv, shift, delta, qacc, kacc, vacc, sems):
    load_keys(near, far, kv, sems)
    tops = stats[0, :SLOTS]
    for part in range(1, GB):
        tops = jnp.maximum(tops, stats[part, :SLOTS])
    totals = jnp.zeros_like(tops)
    deltas = jnp.zeros_like(tops)
    sums = jnp.zeros((8, DH), jnp.float32)
    for part in range(GB):
        weight = jnp.exp2(stats[part, :SLOTS] - tops)
        totals = totals + stats[part, SLOTS : 2 * SLOTS] * weight
        deltas = deltas + stats[part, 2 * SLOTS : 3 * SLOTS] * weight
        sums = sums + stats[part, 3 * SLOTS :]
    latent[...] = sums
    tops = tops + jnp.log2(totals)
    deltas = deltas / totals
    for at in range(SLOTS):
        shift[at] = tops[at : at + 1]
        delta[at] = deltas[at : at + 1]
    qacc[...] = jnp.zeros_like(qacc)
    kacc[...] = jnp.zeros_like(kacc)
    vacc[...] = jnp.zeros_like(vacc)

    def step(p, carry):
        found = []
        for head in range(HEADS):
            for u in range(2):
                row, col, query, grad, key, scores, grad_scores = pair_of(lists, head, 2 * p + u, qg, kv)
                rat, cat = head * GB + row, head * GB + col
                weights = jnp.exp2(scores - shift[rat])
                dscore = (weights * (grad_scores - delta[rat])).astype(jnp.bfloat16)
                weights_low = weights.astype(jnp.bfloat16)
                found.append(
                    (
                        rat,
                        cat,
                        dot(dscore, key, ((0,), (0,))),
                        dot(dscore, query, ((1,), (0,))),
                        dot(weights_low, grad, ((1,), (0,))),
                    )
                )
        for rat, cat, qterm, kterm, vterm in found:
            qacc[rat] += qterm
            kacc[cat] += kterm
            vacc[cat] += vterm
        return carry

    lax.fori_loop(0, lists[2 * HEADS, 0] // 2, step, 0)
    for slot in range(GB):
        for head in range(HEADS):
            at, lanes = head * GB + slot, slice(head * DH, head * DH + DH)
            more = slice(WIDE + head * DH, WIDE + head * DH + DH)
            kvout = kvnear if slot < 8 else kvfar
            qout[slot, :, lanes] = qacc[at].astype(jnp.bfloat16)
            kvout[slot % 8, :, lanes] = kacc[at].astype(jnp.bfloat16)
            kvout[slot % 8, :, more] = vacc[at].astype(jnp.bfloat16)


def shape(*dims, dtype=jnp.bfloat16):
    return jax.ShapeDtypeStruct(dims, dtype)


def body(queries, keys, values, out_grad, token_error, block_mask):
    pair_side = lax.axis_index("pair")
    token_count = token_error.shape[1] * lax.axis_size("qb") * lax.axis_size("kb")
    qg, kv = pl.pallas_call(
        pack_kernel,
        out_shape=(shape(BLK, 2 * WIDE), shape(8, ROWS, 2 * WIDE)),
        in_specs=[VMEM] * 5,
        out_specs=(VMEM, VMEM),
        name="pack",
    )(queries, keys, values, out_grad, token_error)
    side = (lax.axis_index("qb") // 8).astype(jnp.int32).reshape(1)
    lists = pl.pallas_call(
        list_kernel,
        out_shape=shape(2 * HEADS + 1, LIST, dtype=jnp.int32),
        in_specs=[SMEM, SMEM],
        out_specs=SMEM,
        name="pair_lists",
    )(block_mask, side)
    near = lax.all_to_all(kv, "qb", 0, 0, axis_index_groups=Z_GROUPS)
    qg = lax.all_gather(qg, "kb", axis_index_groups=Y_GROUPS)
    far = lax.ppermute(near, "qb", Y_PAIRS)
    qg = lax.all_to_all(
        jnp.broadcast_to(qg[None], (4, 4, BLK, 2 * WIDE)), "kb", 0, 0, axis_index_groups=X_GROUPS
    ).reshape(GB, BLK, 2 * WIDE)

    row_scratch = pltpu.VMEM((SLOTS, 1, DH), jnp.float32)
    block_scratch = pltpu.VMEM((SLOTS, BLK, DH), jnp.float32)
    kv_scratch = pltpu.VMEM((GB, ROWS, 2 * WIDE), jnp.bfloat16)
    copies = pltpu.SemaphoreType.DMA((2,))
    stat = pl.pallas_call(
        stat_kernel,
        out_shape=shape(STAT, DH, dtype=jnp.float32),
        in_specs=[SMEM, VMEM, ANY, ANY],
        out_specs=VMEM,
        scratch_shapes=[kv_scratch, row_scratch, row_scratch, row_scratch, copies],
        compiler_params=PARAMS,
        name="row_stats",
    )(lists, qg, near, far)
    stats = lax.all_to_all(jnp.broadcast_to(stat[None], (GB, STAT, DH)), "kb", 0, 0)
    qpart, kvnear, kvfar, latent = pl.pallas_call(
        grad_kernel,
        out_shape=(
            shape(GB, BLK, WIDE),
            shape(8, BLK, 2 * WIDE),
            shape(8, BLK, 2 * WIDE),
            shape(8, DH, dtype=jnp.float32),
        ),
        in_specs=[SMEM, VMEM, ANY, ANY, VMEM],
        out_specs=(VMEM,) * 4,
        scratch_shapes=[kv_scratch, row_scratch, row_scratch, block_scratch, block_scratch, block_scratch, copies],
        compiler_params=PARAMS,
        name="grads",
    )(lists, qg, near, far, stats)

    own_latent = latent[0, 0]
    partner = lax.ppermute(latent, "pair", [(0, 1), (1, 0)])[0, 0]
    winner_mean = jnp.where(pair_side == 0, own_latent, partner) / token_count
    loser_mean = jnp.where(pair_side == 0, partner, own_latent) / token_count
    keep_share = jax.nn.sigmoid(-beta_pref * (loser_mean - winner_mean))
    factor = jnp.where(pair_side == 0, 1.0 + beta_pref * keep_share, -beta_pref * keep_share)

    kvmore = lax.ppermute(kvfar, "qb", Y_PAIRS)
    qpart = lax.all_to_all(qpart.reshape(4, 4, BLK, WIDE), "kb", 0, 0, axis_index_groups=X_GROUPS)
    qpart = jnp.sum(qpart.astype(jnp.float32), axis=0).astype(jnp.bfloat16)
    kvpart = (kvnear.astype(jnp.float32) + kvmore.astype(jnp.float32)).astype(jnp.bfloat16)
    kvpart = lax.all_to_all(kvpart, "qb", 0, 0, axis_index_groups=Z_GROUPS)
    qpart = lax.all_to_all(qpart, "kb", 0, 0, axis_index_groups=Y_GROUPS)
    kvsum = jnp.sum(kvpart.astype(jnp.float32), axis=0, keepdims=True) * factor
    qsum = jnp.sum(qpart.astype(jnp.float32), axis=0, keepdims=True)
    query_grad = (qsum * (factor * score_scale)).astype(jnp.bfloat16)
    key_grad = (kvsum[..., :WIDE] * score_scale).astype(jnp.bfloat16)
    value_grad = kvsum[..., WIDE:].astype(jnp.bfloat16)
    return (query_grad, key_grad, value_grad)


def solution(mesh):
    return jax.shard_map(
        body,
        mesh=mesh,
        in_specs=(
            P("pair", ("qb", "kb"), None),
            P("pair", ("kb", "qb"), None),
            P("pair", ("kb", "qb"), None),
            P("pair", ("qb", "kb"), None),
            P("pair", ("qb", "kb")),
            P(None, "qb", "kb"),
        ),
        out_specs=(
            P("pair", ("qb", "kb"), None),
            P("pair", ("kb", "qb"), None),
            P("pair", ("kb", "qb"), None),
        ),
        check_vma=False,
    )
```

```python
import jax
import jax.numpy as jnp
from jax import lax
from jax.experimental import pallas as pl
from jax.experimental.pallas import tpu as pltpu
from jax.sharding import PartitionSpec as P

DH = 128
HEADS = 2
BLK = 128
GB = 16
WIDE = HEADS * DH
ROWS = BLK + 16
SLOTS = HEADS * GB
STAT = 3 * SLOTS + 8
LIST = 40

beta_pref = 20.0
neg_big = -1e30
score_scale = DH ** (-0.5)
log2_scale = score_scale * 1.4426950408889634

Y_GROUPS = [[x + 4 * y for y in range(4)] for x in range(4)]
X_GROUPS = [[x + 4 * y for x in range(4)] for y in range(4)]
Z_GROUPS = [[z + 8 * y for z in range(8)] for y in range(2)]
Y_PAIRS = [(s, s ^ 8) for s in range(16)]

VMEM = pl.BlockSpec(memory_space=pltpu.VMEM)
SMEM = pl.BlockSpec(memory_space=pltpu.SMEM)
PARAMS = pltpu.CompilerParams(vmem_limit_bytes=40 * 1024 * 1024)


def dot(a, b, dims):
    return lax.dot_general(a, b, (dims, ((), ())), preferred_element_type=jnp.float32)


def pack_kernel(queries, keys, values, out_grad, token_error, qg_ref, kv_ref):
    qg_ref[:, :WIDE] = queries[0]
    qg_ref[:, WIDE:] = out_grad[0]
    total = jnp.sum(token_error[...], axis=1, keepdims=True)
    high = total.astype(jnp.bfloat16).astype(jnp.float32)
    rest = total - high
    middle = rest.astype(jnp.bfloat16).astype(jnp.float32)
    low = rest - middle
    row = lax.broadcasted_iota(jnp.int32, (16, 2 * WIDE), 0)
    sums = jnp.where(row == 0, high, jnp.where(row == 1, middle, jnp.where(row == 2, low, 0.0)))
    kv_ref[:BLK, :WIDE] = keys[0]
    kv_ref[:BLK, WIDE:] = values[0]
    kv_ref[BLK:, :] = sums.astype(jnp.bfloat16)


def list_kernel(mask, side, lists):
    flip = side[0]
    for head in range(HEADS):

        def step(row, count):
            first = ((row & 3) * 4 + (row >> 2)) * GB
            for col in range(GB):
                lists[head, count] = first + (2 * (col % 8) + ((col // 8) ^ flip))
                count = jnp.minimum(count + mask[head, row, col], LIST - 1)
            return count

        lists[HEADS, head] = lax.fori_loop(0, GB, step, 0)


def pair_of(lists, head, at, qg, kv):
    both = lists[head, at]
    row, col = both >> 4, both & 15
    first, second = head * DH, WIDE + head * DH
    query, grad = qg[row, :, first : first + DH], qg[row, :, second : second + DH]
    key, value = kv[col, :BLK, first : first + DH], kv[col, :BLK, second : second + DH]
    scores = dot(key, query, ((1,), (1,))) * log2_scale
    grad_scores = dot(value, grad, ((1,), (1,)))
    return row, col, query, grad, scores, grad_scores


def stat_kernel(lists, qg, kv, stats, top, total, delta):
    top[...] = jnp.full_like(top, neg_big)
    total[...] = jnp.zeros_like(total)
    delta[...] = jnp.zeros_like(delta)

    def step(p, carry):
        found = []
        for head in range(HEADS):
            for u in range(2):
                row, _, _, _, scores, grad_scores = pair_of(lists, head, 2 * p + u, qg, kv)
                own_top = jnp.max(scores, axis=0, keepdims=True)
                shifted = jnp.exp2(scores - own_top)
                own_total = jnp.sum(shifted, axis=0, keepdims=True)
                own_delta = jnp.sum(shifted * grad_scores, axis=0, keepdims=True)
                found.append((head * GB + row, own_top, own_total, own_delta))
        for at, own_top, own_total, own_delta in found:
            old_top = top[at]
            new_top = jnp.maximum(old_top, own_top)
            old_weight = jnp.exp2(old_top - new_top)
            own_weight = jnp.exp2(own_top - new_top)
            top[at] = new_top
            total[at] = total[at] * old_weight + own_total * own_weight
            delta[at] = delta[at] * old_weight + own_delta * own_weight
        return carry

    lax.fori_loop(0, lists[HEADS, 0] // 2, step, 0)
    for at in range(SLOTS):
        stats[0, at : at + 1, :] = top[at]
        stats[0, SLOTS + at : SLOTS + at + 1, :] = total[at]
        stats[0, 2 * SLOTS + at : 2 * SLOTS + at + 1, :] = delta[at]
    sums = kv[0, BLK:, :DH].astype(jnp.float32)
    for slot in range(1, GB):
        sums = sums + kv[slot, BLK:, :DH].astype(jnp.float32)
    sums = jnp.sum(sums, axis=0, keepdims=True)
    stats[0, 3 * SLOTS :, :] = jnp.broadcast_to(sums, (8, DH))
    own = stats[0]
    for part in range(1, GB):
        stats[part] = own


def key_kernel(lists, qg, kv, stats, kvout, dscores, latent, shift, delta, kacc, vacc):
    tops = stats[0, :SLOTS]
    for part in range(1, GB):
        tops = jnp.maximum(tops, stats[part, :SLOTS])
    totals = jnp.zeros_like(tops)
    deltas = jnp.zeros_like(tops)
    sums = jnp.zeros((8, DH), jnp.float32)
    for part in range(GB):
        weight = jnp.exp2(stats[part, :SLOTS] - tops)
        totals = totals + stats[part, SLOTS : 2 * SLOTS] * weight
        deltas = deltas + stats[part, 2 * SLOTS : 3 * SLOTS] * weight
        sums = sums + stats[part, 3 * SLOTS :]
    latent[...] = sums
    tops = tops + jnp.log2(totals)
    deltas = deltas / totals
    for at in range(SLOTS):
        shift[at] = tops[at : at + 1]
        delta[at] = deltas[at : at + 1]
    kacc[...] = jnp.zeros_like(kacc)
    vacc[...] = jnp.zeros_like(vacc)

    def step(p, carry):
        found = []
        for head in range(HEADS):
            for u in range(2):
                row, col, query, grad, scores, grad_scores = pair_of(lists, head, 2 * p + u, qg, kv)
                rat, cat = head * GB + row, head * GB + col
                weights = jnp.exp2(scores - shift[rat])
                dscore = (weights * (grad_scores - delta[rat])).astype(jnp.bfloat16)
                weights_low = weights.astype(jnp.bfloat16)
                dscores[head, 2 * p + u] = dscore
                found.append((cat, dot(dscore, query, ((1,), (0,))), dot(weights_low, grad, ((1,), (0,)))))
        for cat, kterm, vterm in found:
            kacc[cat] += kterm
            vacc[cat] += vterm
        return carry

    lax.fori_loop(0, lists[HEADS, 0] // 2, step, 0)
    for slot in range(GB):
        for head in range(HEADS):
            first, second = head * DH, WIDE + head * DH
            kvout[slot, :, first : first + DH] = kacc[head * GB + slot].astype(jnp.bfloat16)
            kvout[slot, :, second : second + DH] = vacc[head * GB + slot].astype(jnp.bfloat16)


def query_kernel(lists, kv, dscores, qout, qacc):
    qacc[...] = jnp.zeros_like(qacc)

    def step(p, carry):
        found = []
        for head in range(HEADS):
            for u in range(2):
                both = lists[head, 2 * p + u]
                key = kv[both & 15, :BLK, head * DH : head * DH + DH]
                found.append((head * GB + (both >> 4), dot(dscores[head, 2 * p + u], key, ((0,), (0,)))))
        for rat, qterm in found:
            qacc[rat] += qterm
        return carry

    lax.fori_loop(0, lists[HEADS, 0] // 2, step, 0)
    for slot in range(GB):
        for head in range(HEADS):
            qout[slot, :, head * DH : head * DH + DH] = qacc[head * GB + slot].astype(jnp.bfloat16)


def shape(*dims, dtype=jnp.bfloat16):
    return jax.ShapeDtypeStruct(dims, dtype)


def body(queries, keys, values, out_grad, token_error, block_mask):
    pair_side = lax.axis_index("pair")
    token_count = token_error.shape[1] * lax.axis_size("qb") * lax.axis_size("kb")
    qg, kv = pl.pallas_call(
        pack_kernel,
        out_shape=(shape(BLK, 2 * WIDE), shape(ROWS, 2 * WIDE)),
        in_specs=[VMEM] * 5,
        out_specs=(VMEM, VMEM),
        name="pack",
    )(queries, keys, values, out_grad, token_error)
    side = (lax.axis_index("qb") // 8).astype(jnp.int32).reshape(1)
    lists = pl.pallas_call(
        list_kernel,
        out_shape=shape(HEADS + 1, LIST, dtype=jnp.int32),
        in_specs=[SMEM, SMEM],
        out_specs=SMEM,
        name="pair_lists",
    )(block_mask, side)
    far = lax.ppermute(kv, "qb", Y_PAIRS)
    kv = lax.all_gather(jnp.stack([kv, far]), "qb", axis_index_groups=Z_GROUPS).reshape(GB, ROWS, 2 * WIDE)
    qg = lax.all_gather(qg, "kb", axis_index_groups=Y_GROUPS)
    qg = lax.all_to_all(
        jnp.broadcast_to(qg[None], (4, 4, BLK, 2 * WIDE)), "kb", 0, 0, axis_index_groups=X_GROUPS
    ).reshape(GB, BLK, 2 * WIDE)

    row_scratch = pltpu.VMEM((SLOTS, 1, DH), jnp.float32)
    block_scratch = pltpu.VMEM((SLOTS, BLK, DH), jnp.float32)
    stats = pl.pallas_call(
        stat_kernel,
        out_shape=shape(GB, STAT, DH, dtype=jnp.float32),
        in_specs=[SMEM, VMEM, VMEM],
        out_specs=VMEM,
        scratch_shapes=[row_scratch, row_scratch, row_scratch],
        compiler_params=PARAMS,
        name="row_stats",
    )(lists, qg, kv)
    stats = lax.all_to_all(stats, "kb", 0, 0)
    kvpart, dscores, latent = pl.pallas_call(
        key_kernel,
        out_shape=(
            shape(GB, BLK, 2 * WIDE),
            shape(HEADS, 2 * GB, BLK, BLK),
            shape(8, DH, dtype=jnp.float32),
        ),
        in_specs=[SMEM, VMEM, VMEM, VMEM],
        out_specs=(VMEM,) * 3,
        scratch_shapes=[row_scratch, row_scratch, block_scratch, block_scratch],
        compiler_params=PARAMS,
        name="key_value_grads",
    )(lists, qg, kv, stats)
    kvpart = lax.psum_scatter(
        kvpart.reshape(8, 2 * BLK, 2 * WIDE), "qb", scatter_dimension=0, axis_index_groups=Z_GROUPS
    )
    qpart = pl.pallas_call(
        query_kernel,
        out_shape=shape(GB, BLK, WIDE),
        in_specs=[SMEM, VMEM, VMEM],
        out_specs=VMEM,
        scratch_shapes=[block_scratch],
        compiler_params=PARAMS,
        name="query_grads",
    )(lists, kv, dscores)

    own_latent = latent[0, 0]
    partner = lax.ppermute(latent, "pair", [(0, 1), (1, 0)])[0, 0]
    winner_mean = jnp.where(pair_side == 0, own_latent, partner) / token_count
    loser_mean = jnp.where(pair_side == 0, partner, own_latent) / token_count
    keep_share = jax.nn.sigmoid(-beta_pref * (loser_mean - winner_mean))
    factor = jnp.where(pair_side == 0, 1.0 + beta_pref * keep_share, -beta_pref * keep_share)

    qpart = lax.all_to_all(qpart.reshape(4, 4, BLK, WIDE), "kb", 0, 0, axis_index_groups=X_GROUPS)
    qpart = jnp.sum(qpart.astype(jnp.float32), axis=0).astype(jnp.bfloat16)
    qpart = lax.all_to_all(qpart, "kb", 0, 0, axis_index_groups=Y_GROUPS)
    qsum = jnp.sum(qpart.astype(jnp.float32), axis=0, keepdims=True)
    query_grad = (qsum * (factor * score_scale)).astype(jnp.bfloat16)

    far = lax.ppermute(kvpart[BLK:], "qb", Y_PAIRS)
    kvsum = (kvpart[:BLK].astype(jnp.float32) + far.astype(jnp.float32))[None] * factor
    key_grad = (kvsum[..., :WIDE] * score_scale).astype(jnp.bfloat16)
    value_grad = kvsum[..., WIDE:].astype(jnp.bfloat16)
    return (query_grad, key_grad, value_grad)


def solution(mesh):
    return jax.shard_map(
        body,
        mesh=mesh,
        in_specs=(
            P("pair", ("qb", "kb"), None),
            P("pair", ("kb", "qb"), None),
            P("pair", ("kb", "qb"), None),
            P("pair", ("qb", "kb"), None),
            P("pair", ("qb", "kb")),
            P(None, "qb", "kb"),
        ),
        out_specs=(
            P("pair", ("qb", "kb"), None),
            P("pair", ("kb", "qb"), None),
            P("pair", ("kb", "qb"), None),
        ),
        check_vma=False,
    )
```

```python
import jax
import jax.numpy as jnp
from jax import lax
from jax.experimental import pallas as pl
from jax.experimental.pallas import tpu as pltpu
from jax.sharding import PartitionSpec as P

DH = 128
HEADS = 2
BLK = 128
GB = 16
WIDE = HEADS * DH
ROWS = BLK + 16
SLOTS = HEADS * GB
STAT = 3 * SLOTS + 8
LIST = 40

beta_pref = 20.0
neg_big = -1e30
score_scale = DH ** (-0.5)
log2_scale = score_scale * 1.4426950408889634

Y_GROUPS = [[x + 4 * y for y in range(4)] for x in range(4)]
X_GROUPS = [[x + 4 * y for x in range(4)] for y in range(4)]
Z_GROUPS = [[z + 8 * y for z in range(8)] for y in range(2)]
Y_PAIRS = [(s, s ^ 8) for s in range(16)]

VMEM = pl.BlockSpec(memory_space=pltpu.VMEM)
SMEM = pl.BlockSpec(memory_space=pltpu.SMEM)
PARAMS = pltpu.CompilerParams(vmem_limit_bytes=28 * 1024 * 1024)


def dot(a, b, dims):
    return lax.dot_general(a, b, (dims, ((), ())), preferred_element_type=jnp.float32)


def pack_kernel(queries, keys, values, out_grad, token_error, qg_ref, kv_ref):
    qg_ref[:, :WIDE] = queries[0]
    qg_ref[:, WIDE:] = out_grad[0]
    total = jnp.sum(token_error[...], axis=1, keepdims=True)
    high = total.astype(jnp.bfloat16).astype(jnp.float32)
    rest = total - high
    middle = rest.astype(jnp.bfloat16).astype(jnp.float32)
    low = rest - middle
    row = lax.broadcasted_iota(jnp.int32, (16, 2 * WIDE), 0)
    sums = jnp.where(row == 0, high, jnp.where(row == 1, middle, jnp.where(row == 2, low, 0.0)))
    kv_ref[:BLK, :WIDE] = keys[0]
    kv_ref[:BLK, WIDE:] = values[0]
    kv_ref[BLK:, :] = sums.astype(jnp.bfloat16)


def list_kernel(mask, side, lists):
    flip = side[0]
    for head in range(HEADS):

        def step(row, count):
            first = ((row & 3) * 4 + (row >> 2)) * GB
            for col in range(GB):
                lists[head, count] = first + (2 * (col % 8) + ((col // 8) ^ flip))
                count = jnp.minimum(count + mask[head, row, col], LIST - 1)
            return count

        lists[HEADS, head] = lax.fori_loop(0, GB, step, 0)


def for_pairs(lists, work):
    count = lists[HEADS, 0]

    def fours(step, carry):
        work([(head, 4 * step + u) for u in range(4) for head in range(HEADS)])
        return carry

    lax.fori_loop(0, count >> 2, fours, 0)

    @pl.when((count & 2) != 0)
    def _():
        first = (count >> 2) * 4
        work([(head, first + u) for u in range(2) for head in range(HEADS)])


def blocks_at(ref, slot, head):
    first, second = head * DH, WIDE + head * DH
    return ref[slot, :BLK, first : first + DH], ref[slot, :BLK, second : second + DH]


def stat_kernel(lists, qg, kv, stats, shifted, grad_scores, tops, top, total, delta):
    top[...] = jnp.full_like(top, neg_big)
    total[...] = jnp.zeros_like(total)
    delta[...] = jnp.zeros_like(delta)

    def work(pairs):
        found = []
        for head, at in pairs:
            both = lists[head, at]
            row, col = both >> 4, both & 15
            query, grad = blocks_at(qg, row, head)
            key, value = blocks_at(kv, col, head)
            scores = dot(key, query, ((1,), (1,))) * log2_scale
            product = dot(value, grad, ((1,), (1,)))
            own_top = jnp.max(scores, axis=0, keepdims=True)
            weights = jnp.exp2(scores - own_top)
            shifted[head, at] = weights
            grad_scores[head, at] = product
            tops[head, at] = own_top
            own_total = jnp.sum(weights, axis=0, keepdims=True)
            own_delta = jnp.sum(weights * product, axis=0, keepdims=True)
            found.append((head * GB + row, own_top, own_total, own_delta))
        for at, own_top, own_total, own_delta in found:
            old_top = top[at]
            new_top = jnp.maximum(old_top, own_top)
            old_weight = jnp.exp2(old_top - new_top)
            own_weight = jnp.exp2(own_top - new_top)
            top[at] = new_top
            total[at] = total[at] * old_weight + own_total * own_weight
            delta[at] = delta[at] * old_weight + own_delta * own_weight

    for_pairs(lists, work)
    for at in range(SLOTS):
        stats[0, at : at + 1, :] = top[at]
        stats[0, SLOTS + at : SLOTS + at + 1, :] = total[at]
        stats[0, 2 * SLOTS + at : 2 * SLOTS + at + 1, :] = delta[at]
    sums = kv[0, BLK:, :DH].astype(jnp.float32)
    for slot in range(1, GB):
        sums = sums + kv[slot, BLK:, :DH].astype(jnp.float32)
    sums = jnp.sum(sums, axis=0, keepdims=True)
    stats[0, 3 * SLOTS :, :] = jnp.broadcast_to(sums, (8, DH))
    own = stats[0]
    for part in range(1, GB):
        stats[part] = own


def key_kernel(
    lists, qg, stats, shifted, grad_scores, own_tops, kvout, dscores, latent, shift, delta, kacc, vacc
):
    tops = stats[0, :SLOTS]
    for part in range(1, GB):
        tops = jnp.maximum(tops, stats[part, :SLOTS])
    totals = jnp.zeros_like(tops)
    deltas = jnp.zeros_like(tops)
    sums = jnp.zeros((8, DH), jnp.float32)
    for part in range(GB):
        weight = jnp.exp2(stats[part, :SLOTS] - tops)
        totals = totals + stats[part, SLOTS : 2 * SLOTS] * weight
        deltas = deltas + stats[part, 2 * SLOTS : 3 * SLOTS] * weight
        sums = sums + stats[part, 3 * SLOTS :]
    latent[...] = sums
    tops = tops + jnp.log2(totals)
    deltas = deltas / totals
    for at in range(SLOTS):
        shift[at] = tops[at : at + 1]
        delta[at] = deltas[at : at + 1]
    kacc[...] = jnp.zeros_like(kacc)
    vacc[...] = jnp.zeros_like(vacc)

    def work(pairs):
        found = []
        for head, at in pairs:
            both = lists[head, at]
            row, col = both >> 4, both & 15
            query, grad = blocks_at(qg, row, head)
            scale = jnp.exp2(own_tops[head, at] - shift[head * GB + row])
            weights = shifted[head, at] * scale
            dscore = (weights * (grad_scores[head, at] - delta[head * GB + row])).astype(jnp.bfloat16)
            dscores[head, at] = dscore
            kterm = dot(dscore, query, ((1,), (0,)))
            vterm = dot(weights.astype(jnp.bfloat16), grad, ((1,), (0,)))
            found.append((head * GB + col, kterm, vterm))
        for at, kterm, vterm in found:
            kacc[at] += kterm
            vacc[at] += vterm

    for_pairs(lists, work)
    for slot in range(GB):
        for head in range(HEADS):
            first, second = head * DH, WIDE + head * DH
            kvout[slot, :, first : first + DH] = kacc[head * GB + slot].astype(jnp.bfloat16)
            kvout[slot, :, second : second + DH] = vacc[head * GB + slot].astype(jnp.bfloat16)


def query_kernel(lists, kv, dscores, qout, qacc):
    qacc[...] = jnp.zeros_like(qacc)

    def work(pairs):
        found = []
        for head, at in pairs:
            both = lists[head, at]
            key, _ = blocks_at(kv, both & 15, head)
            found.append((head * GB + (both >> 4), dot(dscores[head, at], key, ((0,), (0,)))))
        for at, qterm in found:
            qacc[at] += qterm

    for_pairs(lists, work)
    for slot in range(GB):
        for head in range(HEADS):
            qout[slot, :, head * DH : head * DH + DH] = qacc[head * GB + slot].astype(jnp.bfloat16)


def shape(*dims, dtype=jnp.bfloat16):
    return jax.ShapeDtypeStruct(dims, dtype)


def body(queries, keys, values, out_grad, token_error, block_mask):
    pair_side = lax.axis_index("pair")
    token_count = token_error.shape[1] * lax.axis_size("qb") * lax.axis_size("kb")
    qg, kv = pl.pallas_call(
        pack_kernel,
        out_shape=(shape(BLK, 2 * WIDE), shape(ROWS, 2 * WIDE)),
        in_specs=[VMEM] * 5,
        out_specs=(VMEM, VMEM),
        name="pack",
    )(queries, keys, values, out_grad, token_error)
    side = (lax.axis_index("qb") // 8).astype(jnp.int32).reshape(1)
    lists = pl.pallas_call(
        list_kernel,
        out_shape=shape(HEADS + 1, LIST, dtype=jnp.int32),
        in_specs=[SMEM, SMEM],
        out_specs=SMEM,
        name="pair_lists",
    )(block_mask, side)
    far = lax.ppermute(kv, "qb", Y_PAIRS)
    kv = lax.all_gather(jnp.stack([kv, far]), "qb", axis_index_groups=Z_GROUPS).reshape(GB, ROWS, 2 * WIDE)
    qg = lax.all_gather(qg, "kb", axis_index_groups=Y_GROUPS)
    qg = lax.all_to_all(
        jnp.broadcast_to(qg[None], (4, 4, BLK, 2 * WIDE)), "kb", 0, 0, axis_index_groups=X_GROUPS
    ).reshape(GB, BLK, 2 * WIDE)

    row_scratch = pltpu.VMEM((SLOTS, 1, DH), jnp.float32)
    block_scratch = pltpu.VMEM((SLOTS, BLK, DH), jnp.float32)
    by_pair = shape(HEADS, 2 * GB, BLK, BLK, dtype=jnp.float32)
    stats, shifted, grad_scores, tops = pl.pallas_call(
        stat_kernel,
        out_shape=(
            shape(GB, STAT, DH, dtype=jnp.float32),
            by_pair,
            by_pair,
            shape(HEADS, 2 * GB, 1, DH, dtype=jnp.float32),
        ),
        in_specs=[SMEM, VMEM, VMEM],
        out_specs=(VMEM,) * 4,
        scratch_shapes=[row_scratch, row_scratch, row_scratch],
        compiler_params=PARAMS,
        name="row_stats",
    )(lists, qg, kv)
    stats = lax.all_to_all(stats, "kb", 0, 0)
    kvpart, dscores, latent = pl.pallas_call(
        key_kernel,
        out_shape=(
            shape(GB, BLK, 2 * WIDE),
            shape(HEADS, 2 * GB, BLK, BLK),
            shape(8, DH, dtype=jnp.float32),
        ),
        in_specs=[SMEM] + [VMEM] * 5,
        out_specs=(VMEM,) * 3,
        scratch_shapes=[row_scratch, row_scratch, block_scratch, block_scratch],
        compiler_params=PARAMS,
        name="key_value_grads",
    )(lists, qg, stats, shifted, grad_scores, tops)
    kvpart = lax.psum_scatter(
        kvpart.reshape(8, 2 * BLK, 2 * WIDE), "qb", scatter_dimension=0, axis_index_groups=Z_GROUPS
    )
    qpart = pl.pallas_call(
        query_kernel,
        out_shape=shape(GB, BLK, WIDE),
        in_specs=[SMEM, VMEM, VMEM],
        out_specs=VMEM,
        scratch_shapes=[block_scratch],
        compiler_params=PARAMS,
        name="query_grads",
    )(lists, kv, dscores)

    own_latent = latent[0, 0]
    partner = lax.ppermute(latent, "pair", [(0, 1), (1, 0)])[0, 0]
    winner_mean = jnp.where(pair_side == 0, own_latent, partner) / token_count
    loser_mean = jnp.where(pair_side == 0, partner, own_latent) / token_count
    keep_share = jax.nn.sigmoid(-beta_pref * (loser_mean - winner_mean))
    factor = jnp.where(pair_side == 0, 1.0 + beta_pref * keep_share, -beta_pref * keep_share)

    qpart = lax.all_to_all(qpart.reshape(4, 4, BLK, WIDE), "kb", 0, 0, axis_index_groups=X_GROUPS)
    qpart = jnp.sum(qpart.astype(jnp.float32), axis=0).astype(jnp.bfloat16)
    qpart = lax.all_to_all(qpart, "kb", 0, 0, axis_index_groups=Y_GROUPS)
    qsum = jnp.sum(qpart.astype(jnp.float32), axis=0, keepdims=True)
    query_grad = (qsum * (factor * score_scale)).astype(jnp.bfloat16)

    far = lax.ppermute(kvpart[BLK:], "qb", Y_PAIRS)
    kvsum = (kvpart[:BLK].astype(jnp.float32) + far.astype(jnp.float32))[None] * factor
    key_grad = (kvsum[..., :WIDE] * score_scale).astype(jnp.bfloat16)
    value_grad = kvsum[..., WIDE:].astype(jnp.bfloat16)
    return (query_grad, key_grad, value_grad)


def solution(mesh):
    return jax.shard_map(
        body,
        mesh=mesh,
        in_specs=(
            P("pair", ("qb", "kb"), None),
            P("pair", ("kb", "qb"), None),
            P("pair", ("kb", "qb"), None),
            P("pair", ("qb", "kb"), None),
            P("pair", ("qb", "kb")),
            P(None, "qb", "kb"),
        ),
        out_specs=(
            P("pair", ("qb", "kb"), None),
            P("pair", ("kb", "qb"), None),
            P("pair", ("kb", "qb"), None),
        ),
        check_vma=False,
    )
```

```python
import jax
import jax.numpy as jnp
from jax import lax
from jax.experimental import pallas as pl
from jax.experimental.pallas import tpu as pltpu
from jax.sharding import PartitionSpec as P

DH = 128
HEADS = 2
BLK = 128
GB = 16
TOKENS = 32768
WIDE = HEADS * DH
ROWS = BLK + 16
SLOTS = HEADS * GB
STAT = 3 * SLOTS + 8
LIST = 40

beta_pref = 20.0
neg_big = -1e30
score_scale = DH ** (-0.5)
log2_scale = score_scale * 1.4426950408889634

Y_GROUPS = [[x + 4 * y for y in range(4)] for x in range(4)]
X_GROUPS = [[x + 4 * y for x in range(4)] for y in range(4)]
Z_GROUPS = [[z + 8 * y for z in range(8)] for y in range(2)]
Y_PAIRS = [[z, z + 8] for z in range(8)]
Y_SWAP = [(s, s ^ 8) for s in range(16)]

VMEM = pl.BlockSpec(memory_space=pltpu.VMEM)
SMEM = pl.BlockSpec(memory_space=pltpu.SMEM)


def params(megabytes):
    return pltpu.CompilerParams(vmem_limit_bytes=megabytes * 1024 * 1024)


def dot(a, b, dims):
    return lax.dot_general(a, b, (dims, ((), ())), preferred_element_type=jnp.float32)


def pack_kernel(queries, keys, values, out_grad, token_error, qg_ref, kv_ref):
    qg_ref[:, :WIDE] = queries[0]
    qg_ref[:, WIDE:] = out_grad[0]
    total = jnp.sum(token_error[...], axis=1, keepdims=True)
    high = total.astype(jnp.bfloat16).astype(jnp.float32)
    rest = total - high
    middle = rest.astype(jnp.bfloat16).astype(jnp.float32)
    low = rest - middle
    row = lax.broadcasted_iota(jnp.int32, (16, 2 * WIDE), 0)
    sums = jnp.where(row == 0, high, jnp.where(row == 1, middle, jnp.where(row == 2, low, 0.0)))
    kv_ref[:BLK, :WIDE] = keys[0]
    kv_ref[:BLK, WIDE:] = values[0]
    kv_ref[BLK:, :] = sums.astype(jnp.bfloat16)


def list_kernel(mask, side, lists):
    lists[HEADS, 2] = side[0]
    for head in range(HEADS):

        def step(row, count):
            first = ((row & 3) * 4 + (row >> 2)) * GB
            for col in range(GB):
                lists[head, count] = first + 2 * (col % 8) + col // 8
                count = jnp.minimum(count + mask[head, row, col], LIST - 1)
            return count

        lists[HEADS, head] = lax.fori_loop(0, GB, step, 0)


def for_pairs(lists, work):
    count = lists[HEADS, 0]

    def fours(step, carry):
        work([(head, 4 * step + u) for u in range(4) for head in range(HEADS)])
        return carry

    lax.fori_loop(0, count >> 2, fours, 0)

    @pl.when((count & 2) != 0)
    def _():
        first = (count >> 2) * 4
        work([(head, first + u) for u in range(2) for head in range(HEADS)])


def blocks_at(ref, slot, head):
    first, second = head * DH, WIDE + head * DH
    return ref[slot, :BLK, first : first + DH], ref[slot, :BLK, second : second + DH]


def stat_kernel(lists, qg, kv, stats, shifted, grad_scores, tops, top, total, delta):
    top[...] = jnp.full_like(top, neg_big)
    total[...] = jnp.zeros_like(total)
    delta[...] = jnp.zeros_like(delta)

    def work(pairs):
        found = []
        for head, at in pairs:
            both = lists[head, at]
            row, col = both >> 4, both & 15
            query, grad = blocks_at(qg, row, head)
            key, value = blocks_at(kv, col, head)
            scores = dot(key, query, ((1,), (1,))) * log2_scale
            product = dot(value, grad, ((1,), (1,)))
            own_top = jnp.max(scores, axis=0, keepdims=True)
            weights = jnp.exp2(scores - own_top)
            shifted[head, at] = weights
            grad_scores[head, at] = product
            tops[head, at] = own_top
            own_total = jnp.sum(weights, axis=0, keepdims=True)
            own_delta = jnp.sum(weights * product, axis=0, keepdims=True)
            found.append((head * GB + row, own_top, own_total, own_delta))
        for at, own_top, own_total, own_delta in found:
            old_top = top[at]
            new_top = jnp.maximum(old_top, own_top)
            old_weight = jnp.exp2(old_top - new_top)
            own_weight = jnp.exp2(own_top - new_top)
            top[at] = new_top
            total[at] = total[at] * old_weight + own_total * own_weight
            delta[at] = delta[at] * old_weight + own_delta * own_weight

    for_pairs(lists, work)
    for at in range(SLOTS):
        stats[0, at : at + 1, :] = top[at]
        stats[0, SLOTS + at : SLOTS + at + 1, :] = total[at]
        stats[0, 2 * SLOTS + at : 2 * SLOTS + at + 1, :] = delta[at]
    sums = kv[0, BLK:, :DH].astype(jnp.float32)
    for slot in range(1, GB):
        sums = sums + kv[slot, BLK:, :DH].astype(jnp.float32)
    sums = jnp.sum(sums, axis=0, keepdims=True)
    stats[0, 3 * SLOTS :, :] = jnp.broadcast_to(sums, (8, DH))
    own = stats[0]
    for part in range(1, GB):
        stats[part] = own


def key_kernel(
    lists, qg, stats, shifted, grad_scores, own_tops, kvout, dscores, latent, shift, delta, kacc, vacc
):
    tops = stats[0, :SLOTS]
    for part in range(1, GB):
        tops = jnp.maximum(tops, stats[part, :SLOTS])
    totals = jnp.zeros_like(tops)
    deltas = jnp.zeros_like(tops)
    sums = jnp.zeros((8, DH), jnp.float32)
    for part in range(GB):
        weight = jnp.exp2(stats[part, :SLOTS] - tops)
        totals = totals + stats[part, SLOTS : 2 * SLOTS] * weight
        deltas = deltas + stats[part, 2 * SLOTS : 3 * SLOTS] * weight
        sums = sums + stats[part, 3 * SLOTS :]
    latent[...] = sums
    tops = tops + jnp.log2(totals)
    deltas = deltas / totals
    for at in range(SLOTS):
        shift[at] = tops[at : at + 1]
        delta[at] = deltas[at : at + 1]
    kacc[...] = jnp.zeros_like(kacc)
    vacc[...] = jnp.zeros_like(vacc)

    def work(pairs):
        found = []
        for head, at in pairs:
            both = lists[head, at]
            row, col = both >> 4, both & 15
            query, grad = blocks_at(qg, row, head)
            scale = jnp.exp2(own_tops[head, at] - shift[head * GB + row])
            weights = shifted[head, at] * scale
            dscore = (weights * (grad_scores[head, at] - delta[head * GB + row])).astype(jnp.bfloat16)
            dscores[head, at] = dscore
            kterm = dot(dscore, query, ((1,), (0,)))
            vterm = dot(weights.astype(jnp.bfloat16), grad, ((1,), (0,)))
            found.append((head * GB + col, kterm, vterm))
        for at, kterm, vterm in found:
            kacc[at] += kterm
            vacc[at] += vterm

    for_pairs(lists, work)
    for slot in range(GB):
        target = slot // 2 * 2 + ((slot & 1) ^ lists[HEADS, 2])
        for head in range(HEADS):
            first, second = head * DH, WIDE + head * DH
            kvout[target, :, first : first + DH] = kacc[head * GB + slot].astype(jnp.bfloat16)
            kvout[target, :, second : second + DH] = vacc[head * GB + slot].astype(jnp.bfloat16)


def query_kernel(lists, kv, dscores, qout, qacc):
    qacc[...] = jnp.zeros_like(qacc)

    def work(pairs):
        found = []
        for head, at in pairs:
            both = lists[head, at]
            key, _ = blocks_at(kv, both & 15, head)
            found.append((head * GB + (both >> 4), dot(dscores[head, at], key, ((0,), (0,)))))
        for at, qterm in found:
            qacc[at] += qterm

    for_pairs(lists, work)
    for slot in range(GB):
        for head in range(HEADS):
            qout[slot, :, head * DH : head * DH + DH] = qacc[head * GB + slot].astype(jnp.bfloat16)


def shape(*dims, dtype=jnp.bfloat16):
    return jax.ShapeDtypeStruct(dims, dtype)


def body(queries, keys, values, out_grad, token_error, block_mask):
    qg, kv = pl.pallas_call(
        pack_kernel,
        out_shape=(shape(BLK, 2 * WIDE), shape(ROWS, 2 * WIDE)),
        in_specs=[VMEM] * 5,
        out_specs=(VMEM, VMEM),
        name="pack",
    )(queries, keys, values, out_grad, token_error)
    lists = pl.pallas_call(
        list_kernel,
        out_shape=shape(HEADS + 1, LIST, dtype=jnp.int32),
        in_specs=[SMEM, SMEM],
        out_specs=SMEM,
        name="pair_lists",
    )(block_mask, (lax.axis_index("qb") // 8).astype(jnp.int32).reshape(1))
    kv = lax.all_gather(kv, "qb", axis_index_groups=Y_PAIRS)
    kv = lax.all_gather(kv, "qb", axis_index_groups=Z_GROUPS).reshape(GB, ROWS, 2 * WIDE)
    qg = lax.all_gather(qg, "kb", axis_index_groups=Y_GROUPS)
    qg = lax.all_to_all(
        jnp.broadcast_to(qg[None], (4, 4, BLK, 2 * WIDE)), "kb", 0, 0, axis_index_groups=X_GROUPS
    ).reshape(GB, BLK, 2 * WIDE)

    row_scratch = pltpu.VMEM((SLOTS, 1, DH), jnp.float32)
    block_scratch = pltpu.VMEM((SLOTS, BLK, DH), jnp.float32)
    by_pair = shape(HEADS, 2 * GB, BLK, BLK, dtype=jnp.float32)
    stats, shifted, grad_scores, tops = pl.pallas_call(
        stat_kernel,
        out_shape=(
            shape(GB, STAT, DH, dtype=jnp.float32),
            by_pair,
            by_pair,
            shape(HEADS, 2 * GB, 1, DH, dtype=jnp.float32),
        ),
        in_specs=[SMEM, VMEM, VMEM],
        out_specs=(VMEM,) * 4,
        scratch_shapes=[row_scratch, row_scratch, row_scratch],
        compiler_params=params(28),
        name="row_stats",
    )(lists, qg, kv)
    stats = lax.all_to_all(stats, "kb", 0, 0)
    kvpart, dscores, latent = pl.pallas_call(
        key_kernel,
        out_shape=(
            shape(GB, BLK, 2 * WIDE),
            shape(HEADS, 2 * GB, BLK, BLK),
            shape(8, DH, dtype=jnp.float32),
        ),
        in_specs=[SMEM] + [VMEM] * 5,
        out_specs=(VMEM, VMEM, VMEM),
        scratch_shapes=[row_scratch, row_scratch, block_scratch, block_scratch],
        compiler_params=params(28),
        name="key_value_grads",
    )(lists, qg, stats, shifted, grad_scores, tops)
    kvpart = lax.psum_scatter(
        kvpart.reshape(8, 2 * BLK, 2 * WIDE), "qb", scatter_dimension=0, axis_index_groups=Z_GROUPS
    )
    qpart = pl.pallas_call(
        query_kernel,
        out_shape=shape(GB, BLK, WIDE),
        in_specs=[SMEM, VMEM, VMEM],
        out_specs=VMEM,
        scratch_shapes=[block_scratch],
        compiler_params=params(28),
        name="query_grads",
    )(lists, kv, dscores)
    partner = lax.ppermute(latent, "pair", [(0, 1), (1, 0)])
    partner, qpart = lax.optimization_barrier((partner, qpart))
    own, other = latent[0, 0], partner[0, 0]
    pair_side = lax.axis_index("pair")
    winner_mean = jnp.where(pair_side == 0, own, other) / TOKENS
    loser_mean = jnp.where(pair_side == 0, other, own) / TOKENS
    keep_share = jax.nn.sigmoid(-beta_pref * (loser_mean - winner_mean))
    factor = jnp.where(pair_side == 0, 1.0 + beta_pref * keep_share, -beta_pref * keep_share)

    qpart = lax.all_to_all(qpart.reshape(4, 4, BLK, WIDE), "kb", 0, 0, axis_index_groups=X_GROUPS)
    qpart = jnp.sum(qpart.astype(jnp.float32), axis=0).astype(jnp.bfloat16)
    qpart = lax.all_to_all(qpart, "kb", 0, 0, axis_index_groups=Y_GROUPS)
    qsum = jnp.sum(qpart.astype(jnp.float32), axis=0, keepdims=True)
    query_grad = (qsum * (factor * score_scale)).astype(jnp.bfloat16)

    kvpart = kvpart.reshape(2 * BLK, 2 * WIDE)
    far = lax.ppermute(kvpart[BLK:], "qb", Y_SWAP)
    near = kvpart[:BLK]
    ksum = near[None, :, :WIDE].astype(jnp.float32) + far[None, :, :WIDE].astype(jnp.float32)
    vsum = near[None, :, WIDE:].astype(jnp.float32) + far[None, :, WIDE:].astype(jnp.float32)
    key_grad = (ksum * (factor * score_scale)).astype(jnp.bfloat16)
    value_grad = (vsum * factor).astype(jnp.bfloat16)
    return (query_grad, key_grad, value_grad)


def solution(mesh):
    return jax.shard_map(
        body,
        mesh=mesh,
        in_specs=(
            P("pair", ("qb", "kb"), None),
            P("pair", ("kb", "qb"), None),
            P("pair", ("kb", "qb"), None),
            P("pair", ("qb", "kb"), None),
            P("pair", ("qb", "kb")),
            P(None, "qb", "kb"),
        ),
        out_specs=(
            P("pair", ("qb", "kb"), None),
            P("pair", ("kb", "qb"), None),
            P("pair", ("kb", "qb"), None),
        ),
        check_vma=False,
    )
```

```python
import jax
import jax.numpy as jnp
from jax import lax
from jax.experimental import pallas as pl
from jax.experimental.pallas import tpu as pltpu
from jax.sharding import PartitionSpec as P

DH = 128
HEADS = 2
BLK = 128
GB = 16
TOKENS = 32768
WIDE = HEADS * DH
ROWS = BLK + 16
SLOTS = HEADS * GB
STAT = 3 * SLOTS + 8
LIST = 40

beta_pref = 20.0
neg_big = -1e30
score_scale = DH ** (-0.5)
log2_scale = score_scale * 1.4426950408889634

Y_GROUPS = [[x + 4 * y for y in range(4)] for x in range(4)]
X_GROUPS = [[x + 4 * y for x in range(4)] for y in range(4)]
Z_GROUPS = [[z + 8 * y for z in range(8)] for y in range(2)]
Y_PAIRS = [[z, z + 8] for z in range(8)]
Y_SWAP = [(s, s ^ 8) for s in range(16)]

VMEM = pl.BlockSpec(memory_space=pltpu.VMEM)
SMEM = pl.BlockSpec(memory_space=pltpu.SMEM)


def params(megabytes):
    return pltpu.CompilerParams(vmem_limit_bytes=megabytes * 1024 * 1024)


def dot(a, b, dims):
    return lax.dot_general(a, b, (dims, ((), ())), preferred_element_type=jnp.float32)


def pack_kernel(queries, keys, values, out_grad, token_error, qg_ref, kv_ref):
    qg_ref[:, :WIDE] = queries[0]
    qg_ref[:, WIDE:] = out_grad[0]
    total = jnp.sum(token_error[...], axis=1, keepdims=True)
    high = total.astype(jnp.bfloat16).astype(jnp.float32)
    rest = total - high
    middle = rest.astype(jnp.bfloat16).astype(jnp.float32)
    low = rest - middle
    row = lax.broadcasted_iota(jnp.int32, (16, 2 * WIDE), 0)
    sums = jnp.where(row == 0, high, jnp.where(row == 1, middle, jnp.where(row == 2, low, 0.0)))
    kv_ref[:BLK, :WIDE] = keys[0]
    kv_ref[:BLK, WIDE:] = values[0]
    kv_ref[BLK:, :] = sums.astype(jnp.bfloat16)


def list_kernel(mask, side, lists):
    lists[HEADS, 2] = side[0]
    for head in range(HEADS):

        def step(row, count):
            first = ((row & 3) * 4 + (row >> 2)) * GB
            for col in range(GB):
                lists[head, count] = first + 2 * (col % 8) + col // 8
                count = jnp.minimum(count + mask[head, row, col], LIST - 1)
            return count

        lists[HEADS, head] = lax.fori_loop(0, GB, step, 0)


def for_pairs(lists, work, most=4):
    count = lists[HEADS, 0]
    whole = count // most

    def several(step, carry):
        work([(head, most * step + u) for u in range(most) for head in range(HEADS)])
        return carry

    lax.fori_loop(0, whole, several, 0)
    first, rest = whole * most, most // 2
    while rest >= 2:

        @pl.when((count & rest) != 0)
        def _(first=first, rest=rest):
            work([(head, first + u) for u in range(rest) for head in range(HEADS)])

        first, rest = first + (count & rest), rest // 2


def blocks_at(ref, slot, head):
    first, second = head * DH, WIDE + head * DH
    return ref[slot, :BLK, first : first + DH], ref[slot, :BLK, second : second + DH]


def stat_kernel(lists, qg, kv, stats, shifted, grad_scores, tops, top, total, delta):
    top[...] = jnp.full_like(top, neg_big)
    total[...] = jnp.zeros_like(total)
    delta[...] = jnp.zeros_like(delta)

    def work(pairs):
        found = []
        for head, at in pairs:
            both = lists[head, at]
            row, col = both >> 4, both & 15
            query, grad = blocks_at(qg, row, head)
            key, value = blocks_at(kv, col, head)
            scores = dot(key, query, ((1,), (1,))) * log2_scale
            product = dot(value, grad, ((1,), (1,)))
            own_top = jnp.max(scores, axis=0, keepdims=True)
            weights = jnp.exp2(scores - own_top)
            shifted[head, at] = weights
            grad_scores[head, at] = product
            tops[head, at] = own_top
            own_total = jnp.sum(weights, axis=0, keepdims=True)
            own_delta = jnp.sum(weights * product, axis=0, keepdims=True)
            found.append((head * GB + row, own_top, own_total, own_delta))
        for at, own_top, own_total, own_delta in found:
            old_top = top[at]
            new_top = jnp.maximum(old_top, own_top)
            old_weight = jnp.exp2(old_top - new_top)
            own_weight = jnp.exp2(own_top - new_top)
            top[at] = new_top
            total[at] = total[at] * old_weight + own_total * own_weight
            delta[at] = delta[at] * old_weight + own_delta * own_weight

    for_pairs(lists, work, 8)
    for at in range(SLOTS):
        stats[0, at : at + 1, :] = top[at]
        stats[0, SLOTS + at : SLOTS + at + 1, :] = total[at]
        stats[0, 2 * SLOTS + at : 2 * SLOTS + at + 1, :] = delta[at]
    sums = kv[0, BLK:, :DH].astype(jnp.float32)
    for slot in range(1, GB):
        sums = sums + kv[slot, BLK:, :DH].astype(jnp.float32)
    sums = jnp.sum(sums, axis=0, keepdims=True)
    stats[0, 3 * SLOTS :, :] = jnp.broadcast_to(sums, (8, DH))
    own = stats[0]
    for part in range(1, GB):
        stats[part] = own


def key_kernel(
    lists, qg, stats, shifted, grad_scores, own_tops, kvout, latent, shift, delta, kacc, vacc
):
    tops = stats[0, :SLOTS]
    for part in range(1, GB):
        tops = jnp.maximum(tops, stats[part, :SLOTS])
    totals = jnp.zeros_like(tops)
    deltas = jnp.zeros_like(tops)
    sums = jnp.zeros((8, DH), jnp.float32)
    for part in range(GB):
        weight = jnp.exp2(stats[part, :SLOTS] - tops)
        totals = totals + stats[part, SLOTS : 2 * SLOTS] * weight
        deltas = deltas + stats[part, 2 * SLOTS : 3 * SLOTS] * weight
        sums = sums + stats[part, 3 * SLOTS :]
    latent[...] = sums
    tops = tops + jnp.log2(totals)
    deltas = deltas / totals
    for at in range(SLOTS):
        shift[at] = tops[at : at + 1]
        delta[at] = deltas[at : at + 1]
    kacc[...] = jnp.zeros_like(kacc)
    vacc[...] = jnp.zeros_like(vacc)

    def work(pairs):
        found = []
        for head, at in pairs:
            both = lists[head, at]
            row, col = both >> 4, both & 15
            query, grad = blocks_at(qg, row, head)
            scale = jnp.exp2(own_tops[head, at] - shift[head * GB + row])
            weights = shifted[head, at] * scale
            dscore = (weights * (grad_scores[head, at] - delta[head * GB + row])).astype(jnp.bfloat16)
            kterm = dot(dscore, query, ((1,), (0,)))
            vterm = dot(weights.astype(jnp.bfloat16), grad, ((1,), (0,)))
            found.append((head * GB + col, kterm, vterm))
        for at, kterm, vterm in found:
            kacc[at] += kterm
            vacc[at] += vterm

    for_pairs(lists, work)
    for slot in range(GB):
        target = slot // 2 * 2 + ((slot & 1) ^ lists[HEADS, 2])
        for head in range(HEADS):
            first, second = head * DH, WIDE + head * DH
            kvout[target, :, first : first + DH] = kacc[head * GB + slot].astype(jnp.bfloat16)
            kvout[target, :, second : second + DH] = vacc[head * GB + slot].astype(jnp.bfloat16)


def query_kernel(lists, kv, shifted, grad_scores, own_tops, shift, delta, qout, qacc):
    qacc[...] = jnp.zeros_like(qacc)

    def work(pairs):
        found = []
        for head, at in pairs:
            both = lists[head, at]
            key, _ = blocks_at(kv, both & 15, head)
            row = head * GB + (both >> 4)
            scale = jnp.exp2(own_tops[head, at] - shift[row])
            dscore = shifted[head, at] * scale * (grad_scores[head, at] - delta[row])
            found.append((row, dot(dscore.astype(jnp.bfloat16), key, ((0,), (0,)))))
        for at, qterm in found:
            qacc[at] += qterm

    for_pairs(lists, work)
    for slot in range(GB):
        for head in range(HEADS):
            qout[slot, :, head * DH : head * DH + DH] = qacc[head * GB + slot].astype(jnp.bfloat16)


def shape(*dims, dtype=jnp.bfloat16):
    return jax.ShapeDtypeStruct(dims, dtype)


def body(queries, keys, values, out_grad, token_error, block_mask):
    qg, kv = pl.pallas_call(
        pack_kernel,
        out_shape=(shape(BLK, 2 * WIDE), shape(ROWS, 2 * WIDE)),
        in_specs=[VMEM] * 5,
        out_specs=(VMEM, VMEM),
        name="pack",
    )(queries, keys, values, out_grad, token_error)
    lists = pl.pallas_call(
        list_kernel,
        out_shape=shape(HEADS + 1, LIST, dtype=jnp.int32),
        in_specs=[SMEM, SMEM],
        out_specs=SMEM,
        name="pair_lists",
    )(block_mask, (lax.axis_index("qb") // 8).astype(jnp.int32).reshape(1))
    kv = lax.all_gather(kv, "qb", axis_index_groups=Y_PAIRS)
    kv = lax.all_gather(kv, "qb", axis_index_groups=Z_GROUPS).reshape(GB, ROWS, 2 * WIDE)
    qg = lax.all_gather(qg, "kb", axis_index_groups=Y_GROUPS)
    qg = lax.all_to_all(
        jnp.broadcast_to(qg[None], (4, 4, BLK, 2 * WIDE)), "kb", 0, 0, axis_index_groups=X_GROUPS
    ).reshape(GB, BLK, 2 * WIDE)

    row_scratch = pltpu.VMEM((SLOTS, 1, DH), jnp.float32)
    block_scratch = pltpu.VMEM((SLOTS, BLK, DH), jnp.float32)
    by_pair = shape(HEADS, 2 * GB, BLK, BLK, dtype=jnp.float32)
    stats, shifted, grad_scores, tops = pl.pallas_call(
        stat_kernel,
        out_shape=(
            shape(GB, STAT, DH, dtype=jnp.float32),
            by_pair,
            by_pair,
            shape(HEADS, 2 * GB, 1, DH, dtype=jnp.float32),
        ),
        in_specs=[SMEM, VMEM, VMEM],
        out_specs=(VMEM,) * 4,
        scratch_shapes=[row_scratch, row_scratch, row_scratch],
        compiler_params=params(28),
        name="row_stats",
    )(lists, qg, kv)
    stats = lax.all_to_all(stats, "kb", 0, 0)
    kvpart, latent, shift, delta = pl.pallas_call(
        key_kernel,
        out_shape=(
            shape(GB, BLK, 2 * WIDE),
            shape(8, DH, dtype=jnp.float32),
            shape(SLOTS, 1, DH, dtype=jnp.float32),
            shape(SLOTS, 1, DH, dtype=jnp.float32),
        ),
        in_specs=[SMEM] + [VMEM] * 5,
        out_specs=(VMEM,) * 4,
        scratch_shapes=[block_scratch, block_scratch],
        compiler_params=params(28),
        name="key_value_grads",
    )(lists, qg, stats, shifted, grad_scores, tops)
    kvpart = lax.psum_scatter(
        kvpart.reshape(8, 2 * BLK, 2 * WIDE), "qb", scatter_dimension=0, axis_index_groups=Z_GROUPS
    )
    qpart = pl.pallas_call(
        query_kernel,
        out_shape=shape(GB, BLK, WIDE),
        in_specs=[SMEM] + [VMEM] * 6,
        out_specs=VMEM,
        scratch_shapes=[block_scratch],
        compiler_params=params(28),
        name="query_grads",
    )(lists, kv, shifted, grad_scores, tops, shift, delta)
    partner = lax.ppermute(latent, "pair", [(0, 1), (1, 0)])
    own, other = latent[0, 0], partner[0, 0]
    pair_side = lax.axis_index("pair")
    winner_mean = jnp.where(pair_side == 0, own, other) / TOKENS
    loser_mean = jnp.where(pair_side == 0, other, own) / TOKENS
    keep_share = jax.nn.sigmoid(-beta_pref * (loser_mean - winner_mean))
    factor = jnp.where(pair_side == 0, 1.0 + beta_pref * keep_share, -beta_pref * keep_share)

    qpart = lax.all_to_all(qpart.reshape(4, 4, BLK, WIDE), "kb", 0, 0, axis_index_groups=X_GROUPS)
    qpart = jnp.sum(qpart.astype(jnp.float32), axis=0).astype(jnp.bfloat16)
    qpart = lax.all_to_all(qpart, "kb", 0, 0, axis_index_groups=Y_GROUPS)
    qsum = jnp.sum(qpart.astype(jnp.float32), axis=0, keepdims=True)
    query_grad = (qsum * (factor * score_scale)).astype(jnp.bfloat16)

    kvpart = kvpart.reshape(2 * BLK, 2 * WIDE)
    far = lax.ppermute(kvpart[BLK:], "qb", Y_SWAP)
    near = kvpart[:BLK]
    ksum = near[None, :, :WIDE].astype(jnp.float32) + far[None, :, :WIDE].astype(jnp.float32)
    vsum = near[None, :, WIDE:].astype(jnp.float32) + far[None, :, WIDE:].astype(jnp.float32)
    key_grad = (ksum * (factor * score_scale)).astype(jnp.bfloat16)
    value_grad = (vsum * factor).astype(jnp.bfloat16)
    return (query_grad, key_grad, value_grad)


def solution(mesh):
    return jax.shard_map(
        body,
        mesh=mesh,
        in_specs=(
            P("pair", ("qb", "kb"), None),
            P("pair", ("kb", "qb"), None),
            P("pair", ("kb", "qb"), None),
            P("pair", ("qb", "kb"), None),
            P("pair", ("qb", "kb")),
            P(None, "qb", "kb"),
        ),
        out_specs=(
            P("pair", ("qb", "kb"), None),
            P("pair", ("kb", "qb"), None),
            P("pair", ("kb", "qb"), None),
        ),
        check_vma=False,
    )
```

```python
import jax
import jax.numpy as jnp
from jax import lax
from jax.experimental import pallas as pl
from jax.experimental.pallas import tpu as pltpu
from jax.sharding import PartitionSpec as P

DH = 128
HEADS = 2
BLK = 128
GB = 16
TOKENS = 32768
WIDE = HEADS * DH
ROWS = BLK + 16
SLOTS = HEADS * GB
STAT = 3 * SLOTS + 8
LIST = 40

beta_pref = 20.0
neg_big = -1e30
score_scale = DH ** (-0.5)
log2_scale = score_scale * 1.4426950408889634

Y_GROUPS = [[x + 4 * y for y in range(4)] for x in range(4)]
X_GROUPS = [[x + 4 * y for x in range(4)] for y in range(4)]
Z_GROUPS = [[z + 8 * y for z in range(8)] for y in range(2)]
Y_PAIRS = [[z, z + 8] for z in range(8)]
Y_SWAP = [(s, s ^ 8) for s in range(16)]

VMEM = pl.BlockSpec(memory_space=pltpu.VMEM)
SMEM = pl.BlockSpec(memory_space=pltpu.SMEM)


def params(megabytes):
    return pltpu.CompilerParams(vmem_limit_bytes=megabytes * 1024 * 1024)


def dot(a, b, dims):
    return lax.dot_general(a, b, (dims, ((), ())), preferred_element_type=jnp.float32)


def pack_kernel(queries, keys, values, out_grad, token_error, qg_ref, kv_ref):
    qg_ref[:, :WIDE] = queries[0]
    qg_ref[:, WIDE:] = out_grad[0]
    total = jnp.sum(token_error[...], axis=1, keepdims=True)
    high = total.astype(jnp.bfloat16).astype(jnp.float32)
    rest = total - high
    middle = rest.astype(jnp.bfloat16).astype(jnp.float32)
    low = rest - middle
    row = lax.broadcasted_iota(jnp.int32, (16, 2 * WIDE), 0)
    sums = jnp.where(row == 0, high, jnp.where(row == 1, middle, jnp.where(row == 2, low, 0.0)))
    kv_ref[:BLK, :WIDE] = keys[0]
    kv_ref[:BLK, WIDE:] = values[0]
    kv_ref[BLK:, :] = sums.astype(jnp.bfloat16)


def list_kernel(mask, side, lists):
    lists[HEADS, 2] = side[0]
    for head in range(HEADS):

        def step(row, count):
            first = ((row & 3) * 4 + (row >> 2)) * GB
            for col in range(GB):
                lists[head, count] = first + 2 * (col % 8) + col // 8
                count = jnp.minimum(count + mask[head, row, col], LIST - 1)
            return count

        lists[HEADS, head] = lax.fori_loop(0, GB, step, 0)


def for_pairs(lists, work, most=4):
    count = lists[HEADS, 0]
    whole = count // most

    def several(step, carry):
        work([(head, most * step + u) for u in range(most) for head in range(HEADS)])
        return carry

    lax.fori_loop(0, whole, several, 0)
    first, rest = whole * most, most // 2
    while rest >= 2:

        @pl.when((count & rest) != 0)
        def _(first=first, rest=rest):
            work([(head, first + u) for u in range(rest) for head in range(HEADS)])

        first, rest = first + (count & rest), rest // 2


def blocks_at(ref, slot, head):
    first, second = head * DH, WIDE + head * DH
    return ref[slot, :BLK, first : first + DH], ref[slot, :BLK, second : second + DH]


def stat_kernel(lists, qg, kv, stats, shifted, grad_scores, tops, top, total, delta):
    top[...] = jnp.full_like(top, neg_big)
    total[...] = jnp.zeros_like(total)
    delta[...] = jnp.zeros_like(delta)

    def work(pairs):
        found = []
        for head, at in pairs:
            both = lists[head, at]
            row, col = both >> 4, both & 15
            query, grad = blocks_at(qg, row, head)
            key, value = blocks_at(kv, col, head)
            scores = dot(key, query, ((1,), (1,))) * log2_scale
            product = dot(value, grad, ((1,), (1,)))
            own_top = jnp.max(scores, axis=0, keepdims=True)
            weights = jnp.exp2(scores - own_top)
            shifted[head, at] = weights
            grad_scores[head, at] = product
            tops[head, at] = own_top
            own_total = jnp.sum(weights, axis=0, keepdims=True)
            own_delta = jnp.sum(weights * product, axis=0, keepdims=True)
            found.append((head * GB + row, own_top, own_total, own_delta))
        for at, own_top, own_total, own_delta in found:
            old_top = top[at]
            new_top = jnp.maximum(old_top, own_top)
            old_weight = jnp.exp2(old_top - new_top)
            own_weight = jnp.exp2(own_top - new_top)
            top[at] = new_top
            total[at] = total[at] * old_weight + own_total * own_weight
            delta[at] = delta[at] * old_weight + own_delta * own_weight

    for_pairs(lists, work, 8)
    for at in range(SLOTS):
        stats[0, at : at + 1, :] = top[at]
        stats[0, SLOTS + at : SLOTS + at + 1, :] = total[at]
        stats[0, 2 * SLOTS + at : 2 * SLOTS + at + 1, :] = delta[at]
    sums = kv[0, BLK:, :DH].astype(jnp.float32)
    for slot in range(1, GB):
        sums = sums + kv[slot, BLK:, :DH].astype(jnp.float32)
    sums = jnp.sum(sums, axis=0, keepdims=True)
    stats[0, 3 * SLOTS :, :] = jnp.broadcast_to(sums, (8, DH))
    own = stats[0]
    for part in range(1, 4):
        stats[part] = own


def merge_kernel(stats, merged):
    tops = stats[0, :SLOTS]
    for part in range(1, 4):
        tops = jnp.maximum(tops, stats[part, :SLOTS])
    totals = jnp.zeros_like(tops)
    deltas = jnp.zeros_like(tops)
    sums = jnp.zeros((8, DH), jnp.float32)
    for part in range(4):
        weight = jnp.exp2(stats[part, :SLOTS] - tops)
        totals = totals + stats[part, SLOTS : 2 * SLOTS] * weight
        deltas = deltas + stats[part, 2 * SLOTS : 3 * SLOTS] * weight
        sums = sums + stats[part, 3 * SLOTS :]
    for part in range(4):
        merged[part, :SLOTS] = tops
        merged[part, SLOTS : 2 * SLOTS] = totals
        merged[part, 2 * SLOTS : 3 * SLOTS] = deltas
        merged[part, 3 * SLOTS :] = sums


def key_kernel(
    lists, qg, stats, shifted, grad_scores, own_tops, kvout, latent, shift, delta, kacc, vacc
):
    tops = stats[0, :SLOTS]
    for part in range(1, 4):
        tops = jnp.maximum(tops, stats[part, :SLOTS])
    totals = jnp.zeros_like(tops)
    deltas = jnp.zeros_like(tops)
    sums = jnp.zeros((8, DH), jnp.float32)
    for part in range(4):
        weight = jnp.exp2(stats[part, :SLOTS] - tops)
        totals = totals + stats[part, SLOTS : 2 * SLOTS] * weight
        deltas = deltas + stats[part, 2 * SLOTS : 3 * SLOTS] * weight
        sums = sums + stats[part, 3 * SLOTS :]
    latent[...] = sums
    tops = tops + jnp.log2(totals)
    deltas = deltas / totals
    for at in range(SLOTS):
        shift[at] = tops[at : at + 1]
        delta[at] = deltas[at : at + 1]
    kacc[...] = jnp.zeros_like(kacc)
    vacc[...] = jnp.zeros_like(vacc)

    def work(pairs):
        found = []
        for head, at in pairs:
            both = lists[head, at]
            row, col = both >> 4, both & 15
            query, grad = blocks_at(qg, row, head)
            scale = jnp.exp2(own_tops[head, at] - shift[head * GB + row])
            weights = shifted[head, at] * scale
            dscore = (weights * (grad_scores[head, at] - delta[head * GB + row])).astype(jnp.bfloat16)
            kterm = dot(dscore, query, ((1,), (0,)))
            vterm = dot(weights.astype(jnp.bfloat16), grad, ((1,), (0,)))
            found.append((head * GB + col, kterm, vterm))
        for at, kterm, vterm in found:
            kacc[at] += kterm
            vacc[at] += vterm

    for_pairs(lists, work)
    for slot in range(GB):
        target = slot // 2 * 2 + ((slot & 1) ^ lists[HEADS, 2])
        for head in range(HEADS):
            first, second = head * DH, WIDE + head * DH
            kvout[target, :, first : first + DH] = kacc[head * GB + slot].astype(jnp.bfloat16)
            kvout[target, :, second : second + DH] = vacc[head * GB + slot].astype(jnp.bfloat16)


def query_kernel(lists, kv, shifted, grad_scores, own_tops, shift, delta, qout, qacc):
    qacc[...] = jnp.zeros_like(qacc)

    def work(pairs):
        found = []
        for head, at in pairs:
            both = lists[head, at]
            key, _ = blocks_at(kv, both & 15, head)
            row = head * GB + (both >> 4)
            scale = jnp.exp2(own_tops[head, at] - shift[row])
            dscore = shifted[head, at] * scale * (grad_scores[head, at] - delta[row])
            found.append((row, dot(dscore.astype(jnp.bfloat16), key, ((0,), (0,)))))
        for at, qterm in found:
            qacc[at] += qterm

    for_pairs(lists, work)
    for slot in range(GB):
        for head in range(HEADS):
            qout[slot, :, head * DH : head * DH + DH] = qacc[head * GB + slot].astype(jnp.bfloat16)


def shape(*dims, dtype=jnp.bfloat16):
    return jax.ShapeDtypeStruct(dims, dtype)


def body(queries, keys, values, out_grad, token_error, block_mask):
    qg, kv = pl.pallas_call(
        pack_kernel,
        out_shape=(shape(BLK, 2 * WIDE), shape(ROWS, 2 * WIDE)),
        in_specs=[VMEM] * 5,
        out_specs=(VMEM, VMEM),
        name="pack",
    )(queries, keys, values, out_grad, token_error)
    lists = pl.pallas_call(
        list_kernel,
        out_shape=shape(HEADS + 1, LIST, dtype=jnp.int32),
        in_specs=[SMEM, SMEM],
        out_specs=SMEM,
        compiler_params=params(4),
        name="pair_lists",
    )(block_mask, (lax.axis_index("qb") // 8).astype(jnp.int32).reshape(1))
    kv = lax.all_gather(kv, "qb", axis_index_groups=Y_PAIRS)
    kv = lax.all_gather(kv, "qb", axis_index_groups=Z_GROUPS).reshape(GB, ROWS, 2 * WIDE)
    qg = lax.all_gather(qg, "kb", axis_index_groups=Y_GROUPS)
    qg = lax.all_to_all(
        jnp.broadcast_to(qg[None], (4, 4, BLK, 2 * WIDE)), "kb", 0, 0, axis_index_groups=X_GROUPS
    ).reshape(GB, BLK, 2 * WIDE)

    row_scratch = pltpu.VMEM((SLOTS, 1, DH), jnp.float32)
    block_scratch = pltpu.VMEM((SLOTS, BLK, DH), jnp.float32)
    by_pair = shape(HEADS, 2 * GB, BLK, BLK, dtype=jnp.float32)
    stats, shifted, grad_scores, tops = pl.pallas_call(
        stat_kernel,
        out_shape=(
            shape(4, STAT, DH, dtype=jnp.float32),
            by_pair,
            by_pair,
            shape(HEADS, 2 * GB, 1, DH, dtype=jnp.float32),
        ),
        in_specs=[SMEM, VMEM, VMEM],
        out_specs=(VMEM,) * 4,
        scratch_shapes=[row_scratch, row_scratch, row_scratch],
        compiler_params=params(28),
        name="row_stats",
    )(lists, qg, kv)
    stats = lax.all_to_all(stats, "kb", 0, 0, axis_index_groups=X_GROUPS)
    stats = pl.pallas_call(
        merge_kernel,
        out_shape=shape(4, STAT, DH, dtype=jnp.float32),
        in_specs=[VMEM],
        out_specs=VMEM,
        compiler_params=params(4),
        name="merge_stats",
    )(stats)
    stats = lax.all_to_all(stats, "kb", 0, 0, axis_index_groups=Y_GROUPS)
    kvpart, latent, shift, delta = pl.pallas_call(
        key_kernel,
        out_shape=(
            shape(GB, BLK, 2 * WIDE),
            shape(8, DH, dtype=jnp.float32),
            shape(SLOTS, 1, DH, dtype=jnp.float32),
            shape(SLOTS, 1, DH, dtype=jnp.float32),
        ),
        in_specs=[SMEM] + [VMEM] * 5,
        out_specs=(VMEM,) * 4,
        scratch_shapes=[block_scratch, block_scratch],
        compiler_params=params(28),
        name="key_value_grads",
    )(lists, qg, stats, shifted, grad_scores, tops)
    kvpart = lax.psum_scatter(
        kvpart.reshape(8, 2 * BLK, 2 * WIDE), "qb", scatter_dimension=0, axis_index_groups=Z_GROUPS
    )
    qpart = pl.pallas_call(
        query_kernel,
        out_shape=shape(GB, BLK, WIDE),
        in_specs=[SMEM] + [VMEM] * 6,
        out_specs=VMEM,
        scratch_shapes=[block_scratch],
        compiler_params=params(28),
        name="query_grads",
    )(lists, kv, shifted, grad_scores, tops, shift, delta)
    partner = lax.ppermute(latent, "pair", [(0, 1), (1, 0)])
    own, other = latent[0, 0], partner[0, 0]
    pair_side = lax.axis_index("pair")
    winner_mean = jnp.where(pair_side == 0, own, other) / TOKENS
    loser_mean = jnp.where(pair_side == 0, other, own) / TOKENS
    keep_share = jax.nn.sigmoid(-beta_pref * (loser_mean - winner_mean))
    factor = jnp.where(pair_side == 0, 1.0 + beta_pref * keep_share, -beta_pref * keep_share)

    qpart = lax.all_to_all(qpart.reshape(4, 4, BLK, WIDE), "kb", 0, 0, axis_index_groups=X_GROUPS)
    qpart = jnp.sum(qpart.astype(jnp.float32), axis=0).astype(jnp.bfloat16)
    qpart = lax.all_to_all(qpart, "kb", 0, 0, axis_index_groups=Y_GROUPS)
    qsum = jnp.sum(qpart.astype(jnp.float32), axis=0, keepdims=True)
    query_grad = (qsum * (factor * score_scale)).astype(jnp.bfloat16)

    kvpart = kvpart.reshape(2 * BLK, 2 * WIDE)
    far = lax.ppermute(kvpart[BLK:], "qb", Y_SWAP)
    near = kvpart[:BLK]
    ksum = near[None, :, :WIDE].astype(jnp.float32) + far[None, :, :WIDE].astype(jnp.float32)
    vsum = near[None, :, WIDE:].astype(jnp.float32) + far[None, :, WIDE:].astype(jnp.float32)
    key_grad = (ksum * (factor * score_scale)).astype(jnp.bfloat16)
    value_grad = (vsum * factor).astype(jnp.bfloat16)
    return (query_grad, key_grad, value_grad)


def solution(mesh):
    return jax.shard_map(
        body,
        mesh=mesh,
        in_specs=(
            P("pair", ("qb", "kb"), None),
            P("pair", ("kb", "qb"), None),
            P("pair", ("kb", "qb"), None),
            P("pair", ("qb", "kb"), None),
            P("pair", ("qb", "kb")),
            P(None, "qb", "kb"),
        ),
        out_specs=(
            P("pair", ("qb", "kb"), None),
            P("pair", ("kb", "qb"), None),
            P("pair", ("kb", "qb"), None),
        ),
        check_vma=False,
    )
```

```python
import jax
import jax.numpy as jnp
from jax import lax
from jax.experimental import pallas as pl
from jax.experimental.pallas import tpu as pltpu
from jax.sharding import PartitionSpec as P

DH = 128
HEADS = 2
BLK = 128
GB = 16
TOKENS = 32768
WIDE = HEADS * DH
ROWS = BLK + 16
SLOTS = HEADS * GB
STAT = 3 * SLOTS + 8
LIST = 40

beta_pref = 20.0
neg_big = -1e30
score_scale = DH ** (-0.5)
log2_scale = score_scale * 1.4426950408889634

Y_GROUPS = [[x + 4 * y for y in range(4)] for x in range(4)]
X_GROUPS = [[x + 4 * y for x in range(4)] for y in range(4)]
Z_GROUPS = [[z + 8 * y for z in range(8)] for y in range(2)]
Y_PAIRS = [[z, z + 8] for z in range(8)]
Y_SWAP = [(s, s ^ 8) for s in range(16)]

VMEM = pl.BlockSpec(memory_space=pltpu.VMEM)
SMEM = pl.BlockSpec(memory_space=pltpu.SMEM)


def params(megabytes):
    return pltpu.CompilerParams(vmem_limit_bytes=megabytes * 1024 * 1024)


def dot(a, b, dims):
    return lax.dot_general(a, b, (dims, ((), ())), preferred_element_type=jnp.float32)


def pack_kernel(queries, keys, values, out_grad, token_error, qg_ref, kv_ref):
    qg_ref[:, :WIDE] = queries[0]
    qg_ref[:, WIDE:] = out_grad[0]
    total = jnp.sum(token_error[...], axis=1, keepdims=True)
    high = total.astype(jnp.bfloat16).astype(jnp.float32)
    rest = total - high
    middle = rest.astype(jnp.bfloat16).astype(jnp.float32)
    low = rest - middle
    row = lax.broadcasted_iota(jnp.int32, (16, 2 * WIDE), 0)
    sums = jnp.where(row == 0, high, jnp.where(row == 1, middle, jnp.where(row == 2, low, 0.0)))
    kv_ref[:BLK, :WIDE] = keys[0]
    kv_ref[:BLK, WIDE:] = values[0]
    kv_ref[BLK:, :] = sums.astype(jnp.bfloat16)


def copies_kernel(source, target, sems):
    copies = [pltpu.make_async_copy(source, target.at[at], sems.at[at]) for at in range(4)]
    for copy in copies:
        copy.start()
    for copy in copies:
        copy.wait()


def list_kernel(mask, side, lists):
    lists[HEADS, 2] = side[0]
    for head in range(HEADS):

        def step(row, count):
            first = ((row & 3) * 4 + (row >> 2)) * GB
            for col in range(GB):
                lists[head, count] = first + 2 * (col % 8) + col // 8
                count = jnp.minimum(count + mask[head, row, col], LIST - 1)
            return count

        lists[HEADS, head] = lax.fori_loop(0, GB, step, 0)


def for_pairs(lists, work, most=4):
    count = lists[HEADS, 0]
    whole = count // most

    def several(step, carry):
        work([(head, most * step + u) for u in range(most) for head in range(HEADS)])
        return carry

    lax.fori_loop(0, whole, several, 0)
    first, rest = whole * most, most // 2
    while rest >= 2:

        @pl.when((count & rest) != 0)
        def _(first=first, rest=rest):
            work([(head, first + u) for u in range(rest) for head in range(HEADS)])

        first, rest = first + (count & rest), rest // 2


def blocks_at(ref, slot, head):
    first, second = head * DH, WIDE + head * DH
    return ref[slot, :BLK, first : first + DH], ref[slot, :BLK, second : second + DH]


def stat_kernel(lists, qg, kv, stats, shifted, grad_scores, tops, top, total, delta):
    top[...] = jnp.full_like(top, neg_big)
    total[...] = jnp.zeros_like(total)
    delta[...] = jnp.zeros_like(delta)

    def work(pairs):
        found = []
        for head, at in pairs:
            both = lists[head, at]
            row, col = both >> 4, both & 15
            query, grad = blocks_at(qg, row, head)
            key, value = blocks_at(kv, col, head)
            scores = dot(key, query, ((1,), (1,))) * log2_scale
            product = dot(value, grad, ((1,), (1,)))
            own_top = jnp.max(scores, axis=0, keepdims=True)
            weights = jnp.exp2(scores - own_top)
            shifted[head, at] = weights
            grad_scores[head, at] = product
            tops[head, at] = own_top
            own_total = jnp.sum(weights, axis=0, keepdims=True)
            own_delta = jnp.sum(weights * product, axis=0, keepdims=True)
            found.append((head * GB + row, own_top, own_total, own_delta))
        for at, own_top, own_total, own_delta in found:
            old_top = top[at]
            new_top = jnp.maximum(old_top, own_top)
            old_weight = jnp.exp2(old_top - new_top)
            own_weight = jnp.exp2(own_top - new_top)
            top[at] = new_top
            total[at] = total[at] * old_weight + own_total * own_weight
            delta[at] = delta[at] * old_weight + own_delta * own_weight

    for_pairs(lists, work, 8)
    for at in range(SLOTS):
        stats[0, at : at + 1, :] = top[at]
        stats[0, SLOTS + at : SLOTS + at + 1, :] = total[at]
        stats[0, 2 * SLOTS + at : 2 * SLOTS + at + 1, :] = delta[at]
    sums = kv[0, BLK:, :DH].astype(jnp.float32)
    for slot in range(1, GB):
        sums = sums + kv[slot, BLK:, :DH].astype(jnp.float32)
    sums = jnp.sum(sums, axis=0, keepdims=True)
    stats[0, 3 * SLOTS :, :] = jnp.broadcast_to(sums, (8, DH))
    own = stats[0]
    for part in range(1, 4):
        stats[part] = own


def merge_kernel(stats, merged):
    tops = stats[0, :SLOTS]
    for part in range(1, 4):
        tops = jnp.maximum(tops, stats[part, :SLOTS])
    totals = jnp.zeros_like(tops)
    deltas = jnp.zeros_like(tops)
    sums = jnp.zeros((8, DH), jnp.float32)
    for part in range(4):
        weight = jnp.exp2(stats[part, :SLOTS] - tops)
        totals = totals + stats[part, SLOTS : 2 * SLOTS] * weight
        deltas = deltas + stats[part, 2 * SLOTS : 3 * SLOTS] * weight
        sums = sums + stats[part, 3 * SLOTS :]
    for part in range(4):
        merged[part, :SLOTS] = tops
        merged[part, SLOTS : 2 * SLOTS] = totals
        merged[part, 2 * SLOTS : 3 * SLOTS] = deltas
        merged[part, 3 * SLOTS :] = sums


def key_kernel(
    lists, qg, stats, shifted, grad_scores, own_tops, kvout, latent, shift, delta, kacc, vacc
):
    tops = stats[0, :SLOTS]
    for part in range(1, 4):
        tops = jnp.maximum(tops, stats[part, :SLOTS])
    totals = jnp.zeros_like(tops)
    deltas = jnp.zeros_like(tops)
    sums = jnp.zeros((8, DH), jnp.float32)
    for part in range(4):
        weight = jnp.exp2(stats[part, :SLOTS] - tops)
        totals = totals + stats[part, SLOTS : 2 * SLOTS] * weight
        deltas = deltas + stats[part, 2 * SLOTS : 3 * SLOTS] * weight
        sums = sums + stats[part, 3 * SLOTS :]
    latent[...] = sums
    tops = tops + jnp.log2(totals)
    deltas = deltas / totals
    for at in range(SLOTS):
        shift[at] = tops[at : at + 1]
        delta[at] = deltas[at : at + 1]
    kacc[...] = jnp.zeros_like(kacc)
    vacc[...] = jnp.zeros_like(vacc)

    def work(pairs):
        found = []
        for head, at in pairs:
            both = lists[head, at]
            row, col = both >> 4, both & 15
            query, grad = blocks_at(qg, row, head)
            scale = jnp.exp2(own_tops[head, at] - shift[head * GB + row])
            weights = shifted[head, at] * scale
            dscore = (weights * (grad_scores[head, at] - delta[head * GB + row])).astype(jnp.bfloat16)
            kterm = dot(dscore, query, ((1,), (0,)))
            vterm = dot(weights.astype(jnp.bfloat16), grad, ((1,), (0,)))
            found.append((head * GB + col, kterm, vterm))
        for at, kterm, vterm in found:
            kacc[at] += kterm
            vacc[at] += vterm

    for_pairs(lists, work)
    for slot in range(GB):
        target = slot // 2 * 2 + ((slot & 1) ^ lists[HEADS, 2])
        for head in range(HEADS):
            first, second = head * DH, WIDE + head * DH
            kvout[target, :, first : first + DH] = kacc[head * GB + slot].astype(jnp.bfloat16)
            kvout[target, :, second : second + DH] = vacc[head * GB + slot].astype(jnp.bfloat16)


def query_kernel(lists, kv, shifted, grad_scores, own_tops, shift, delta, qout, qacc):
    qacc[...] = jnp.zeros_like(qacc)

    def work(pairs):
        found = []
        for head, at in pairs:
            both = lists[head, at]
            key, _ = blocks_at(kv, both & 15, head)
            row = head * GB + (both >> 4)
            scale = jnp.exp2(own_tops[head, at] - shift[row])
            dscore = shifted[head, at] * scale * (grad_scores[head, at] - delta[row])
            found.append((row, dot(dscore.astype(jnp.bfloat16), key, ((0,), (0,)))))
        for at, qterm in found:
            qacc[at] += qterm

    for_pairs(lists, work)
    for slot in range(GB):
        for head in range(HEADS):
            qout[slot, :, head * DH : head * DH + DH] = qacc[head * GB + slot].astype(jnp.bfloat16)


def shape(*dims, dtype=jnp.bfloat16):
    return jax.ShapeDtypeStruct(dims, dtype)


def body(queries, keys, values, out_grad, token_error, block_mask):
    qg, kv = pl.pallas_call(
        pack_kernel,
        out_shape=(shape(BLK, 2 * WIDE), shape(ROWS, 2 * WIDE)),
        in_specs=[VMEM] * 5,
        out_specs=(VMEM, VMEM),
        name="pack",
    )(queries, keys, values, out_grad, token_error)
    lists = pl.pallas_call(
        list_kernel,
        out_shape=shape(HEADS + 1, LIST, dtype=jnp.int32),
        in_specs=[SMEM, SMEM],
        out_specs=SMEM,
        compiler_params=params(4),
        name="pair_lists",
    )(block_mask, (lax.axis_index("qb") // 8).astype(jnp.int32).reshape(1))
    kv = lax.all_gather(kv, "qb", axis_index_groups=Y_PAIRS)
    kv = lax.all_gather(kv, "qb", axis_index_groups=Z_GROUPS).reshape(GB, ROWS, 2 * WIDE)
    qg = lax.all_gather(qg, "kb", axis_index_groups=Y_GROUPS)
    qg = pl.pallas_call(
        copies_kernel,
        out_shape=shape(4, 4, BLK, 2 * WIDE),
        in_specs=[VMEM],
        out_specs=pl.BlockSpec(memory_space=pl.ANY),
        scratch_shapes=[pltpu.SemaphoreType.DMA((4,))],
        compiler_params=params(4),
        name="four_copies",
    )(qg)
    qg = lax.all_to_all(qg, "kb", 0, 0, axis_index_groups=X_GROUPS).reshape(GB, BLK, 2 * WIDE)

    row_scratch = pltpu.VMEM((SLOTS, 1, DH), jnp.float32)
    block_scratch = pltpu.VMEM((SLOTS, BLK, DH), jnp.float32)
    by_pair = shape(HEADS, 2 * GB, BLK, BLK, dtype=jnp.float32)
    stats, shifted, grad_scores, tops = pl.pallas_call(
        stat_kernel,
        out_shape=(
            shape(4, STAT, DH, dtype=jnp.float32),
            by_pair,
            by_pair,
            shape(HEADS, 2 * GB, 1, DH, dtype=jnp.float32),
        ),
        in_specs=[SMEM, VMEM, VMEM],
        out_specs=(VMEM,) * 4,
        scratch_shapes=[row_scratch, row_scratch, row_scratch],
        compiler_params=params(28),
        name="row_stats",
    )(lists, qg, kv)
    stats = lax.all_to_all(stats, "kb", 0, 0, axis_index_groups=X_GROUPS)
    stats = pl.pallas_call(
        merge_kernel,
        out_shape=shape(4, STAT, DH, dtype=jnp.float32),
        in_specs=[VMEM],
        out_specs=VMEM,
        compiler_params=params(4),
        name="merge_stats",
    )(stats)
    stats = lax.all_to_all(stats, "kb", 0, 0, axis_index_groups=Y_GROUPS)
    kvpart, latent, shift, delta = pl.pallas_call(
        key_kernel,
        out_shape=(
            shape(GB, BLK, 2 * WIDE),
            shape(8, DH, dtype=jnp.float32),
            shape(SLOTS, 1, DH, dtype=jnp.float32),
            shape(SLOTS, 1, DH, dtype=jnp.float32),
        ),
        in_specs=[SMEM] + [VMEM] * 5,
        out_specs=(VMEM,) * 4,
        scratch_shapes=[block_scratch, block_scratch],
        compiler_params=params(28),
        name="key_value_grads",
    )(lists, qg, stats, shifted, grad_scores, tops)
    kvpart = lax.psum_scatter(
        kvpart.reshape(8, 2 * BLK, 2 * WIDE), "qb", scatter_dimension=0, axis_index_groups=Z_GROUPS
    )
    qpart = pl.pallas_call(
        query_kernel,
        out_shape=shape(GB, BLK, WIDE),
        in_specs=[SMEM] + [VMEM] * 6,
        out_specs=VMEM,
        scratch_shapes=[block_scratch],
        compiler_params=params(28),
        name="query_grads",
    )(lists, kv, shifted, grad_scores, tops, shift, delta)
    partner = lax.ppermute(latent, "pair", [(0, 1), (1, 0)])
    own, other = latent[0, 0], partner[0, 0]
    pair_side = lax.axis_index("pair")
    winner_mean = jnp.where(pair_side == 0, own, other) / TOKENS
    loser_mean = jnp.where(pair_side == 0, other, own) / TOKENS
    keep_share = jax.nn.sigmoid(-beta_pref * (loser_mean - winner_mean))
    factor = jnp.where(pair_side == 0, 1.0 + beta_pref * keep_share, -beta_pref * keep_share)

    qpart = lax.all_to_all(qpart.reshape(4, 4, BLK, WIDE), "kb", 0, 0, axis_index_groups=X_GROUPS)
    qpart = jnp.sum(qpart.astype(jnp.float32), axis=0).astype(jnp.bfloat16)
    qpart = lax.all_to_all(qpart, "kb", 0, 0, axis_index_groups=Y_GROUPS)
    qsum = jnp.sum(qpart.astype(jnp.float32), axis=0, keepdims=True)
    query_grad = (qsum * (factor * score_scale)).astype(jnp.bfloat16)

    kvpart = kvpart.reshape(2 * BLK, 2 * WIDE)
    far = lax.ppermute(kvpart[BLK:], "qb", Y_SWAP)
    near = kvpart[:BLK]
    ksum = near[None, :, :WIDE].astype(jnp.float32) + far[None, :, :WIDE].astype(jnp.float32)
    vsum = near[None, :, WIDE:].astype(jnp.float32) + far[None, :, WIDE:].astype(jnp.float32)
    key_grad = (ksum * (factor * score_scale)).astype(jnp.bfloat16)
    value_grad = (vsum * factor).astype(jnp.bfloat16)
    return (query_grad, key_grad, value_grad)


def solution(mesh):
    return jax.shard_map(
        body,
        mesh=mesh,
        in_specs=(
            P("pair", ("qb", "kb"), None),
            P("pair", ("kb", "qb"), None),
            P("pair", ("kb", "qb"), None),
            P("pair", ("qb", "kb"), None),
            P("pair", ("qb", "kb")),
            P(None, "qb", "kb"),
        ),
        out_specs=(
            P("pair", ("qb", "kb"), None),
            P("pair", ("kb", "qb"), None),
            P("pair", ("kb", "qb"), None),
        ),
        check_vma=False,
    )
```

```python
import jax
import jax.numpy as jnp
from jax import lax
from jax.experimental import pallas as pl
from jax.experimental.pallas import tpu as pltpu
from jax.sharding import PartitionSpec as P

DH = 128
HEADS = 2
BLK = 128
GB = 16
TOKENS = 32768
WIDE = HEADS * DH
ROWS = BLK + 16
SLOTS = HEADS * GB
STAT = 3 * SLOTS + 8
LIST = 40

beta_pref = 20.0
neg_big = -1e30
score_scale = DH ** (-0.5)
log2_scale = score_scale * 1.4426950408889634

Y_GROUPS = [[x + 4 * y for y in range(4)] for x in range(4)]
X_GROUPS = [[x + 4 * y for x in range(4)] for y in range(4)]
Z_GROUPS = [[z + 8 * y for z in range(8)] for y in range(2)]
Y_PAIRS = [[z, z + 8] for z in range(8)]
Y_SWAP = [(s, s ^ 8) for s in range(16)]

VMEM = pl.BlockSpec(memory_space=pltpu.VMEM)
SMEM = pl.BlockSpec(memory_space=pltpu.SMEM)


def params(megabytes):
    return pltpu.CompilerParams(vmem_limit_bytes=megabytes * 1024 * 1024)


def dot(a, b, dims):
    return lax.dot_general(a, b, (dims, ((), ())), preferred_element_type=jnp.float32)


def pack_kernel(queries, keys, values, out_grad, token_error, qg_ref, kv_ref):
    qg_ref[:, :WIDE] = queries[0]
    qg_ref[:, WIDE:] = out_grad[0]
    total = jnp.sum(token_error[...], axis=1, keepdims=True)
    high = total.astype(jnp.bfloat16).astype(jnp.float32)
    rest = total - high
    middle = rest.astype(jnp.bfloat16).astype(jnp.float32)
    low = rest - middle
    row = lax.broadcasted_iota(jnp.int32, (16, 2 * WIDE), 0)
    sums = jnp.where(row == 0, high, jnp.where(row == 1, middle, jnp.where(row == 2, low, 0.0)))
    kv_ref[:BLK, :WIDE] = keys[0]
    kv_ref[:BLK, WIDE:] = values[0]
    kv_ref[BLK:, :] = sums.astype(jnp.bfloat16)


def copies_kernel(source, target, sems):
    copies = [pltpu.make_async_copy(source, target.at[at], sems.at[at]) for at in range(4)]
    for copy in copies:
        copy.start()
    for copy in copies:
        copy.wait()


def list_kernel(mask, side, lists):
    lists[HEADS, 2] = side[0]
    for head in range(HEADS):

        def step(row, count):
            first = ((row & 3) * 4 + (row >> 2)) * GB
            for col in range(GB):
                lists[head, count] = first + 2 * (col % 8) + col // 8
                count = jnp.minimum(count + mask[head, row, col], LIST - 1)
            return count

        lists[HEADS, head] = lax.fori_loop(0, GB, step, 0)


def for_pairs(lists, work, most=4):
    count = lists[HEADS, 0]
    whole = count // most

    def several(step, carry):
        work([(head, most * step + u) for u in range(most) for head in range(HEADS)])
        return carry

    lax.fori_loop(0, whole, several, 0)
    first, rest = whole * most, most // 2
    while rest >= 2:

        @pl.when((count & rest) != 0)
        def _(first=first, rest=rest):
            work([(head, first + u) for u in range(rest) for head in range(HEADS)])

        first, rest = first + (count & rest), rest // 2


def blocks_at(ref, slot, head):
    first, second = head * DH, WIDE + head * DH
    return ref[slot, :BLK, first : first + DH], ref[slot, :BLK, second : second + DH]


def stat_kernel(lists, qg, kv, stats, shifted, grad_scores, tops, top, total, delta):
    top[...] = jnp.full_like(top, neg_big)
    total[...] = jnp.zeros_like(total)
    delta[...] = jnp.zeros_like(delta)

    def work(pairs):
        found = []
        for head, at in pairs:
            both = lists[head, at]
            row, col = both >> 4, both & 15
            query, grad = blocks_at(qg, row, head)
            key, value = blocks_at(kv, col, head)
            scores = dot(key, query, ((1,), (1,))) * log2_scale
            product = dot(value, grad, ((1,), (1,)))
            own_top = jnp.max(scores, axis=0, keepdims=True)
            weights = jnp.exp2(scores - own_top)
            shifted[head, at] = weights
            grad_scores[head, at] = product
            tops[head, at] = own_top
            own_total = jnp.sum(weights, axis=0, keepdims=True)
            own_delta = jnp.sum(weights * product, axis=0, keepdims=True)
            found.append((head * GB + row, own_top, own_total, own_delta))
        for at, own_top, own_total, own_delta in found:
            old_top = top[at]
            new_top = jnp.maximum(old_top, own_top)
            old_weight = jnp.exp2(old_top - new_top)
            own_weight = jnp.exp2(own_top - new_top)
            top[at] = new_top
            total[at] = total[at] * old_weight + own_total * own_weight
            delta[at] = delta[at] * old_weight + own_delta * own_weight

    for_pairs(lists, work, 8)
    for at in range(SLOTS):
        stats[0, at : at + 1, :] = top[at]
        stats[0, SLOTS + at : SLOTS + at + 1, :] = total[at]
        stats[0, 2 * SLOTS + at : 2 * SLOTS + at + 1, :] = delta[at]
    sums = kv[0, BLK:, :DH].astype(jnp.float32)
    for slot in range(1, GB):
        sums = sums + kv[slot, BLK:, :DH].astype(jnp.float32)
    sums = jnp.sum(sums, axis=0, keepdims=True)
    stats[0, 3 * SLOTS :, :] = jnp.broadcast_to(sums, (8, DH))
    own = stats[0]
    for part in range(1, 4):
        stats[part] = own


def merge_kernel(stats, merged):
    tops = stats[0, :SLOTS]
    for part in range(1, 4):
        tops = jnp.maximum(tops, stats[part, :SLOTS])
    totals = jnp.zeros_like(tops)
    deltas = jnp.zeros_like(tops)
    sums = jnp.zeros((8, DH), jnp.float32)
    for part in range(4):
        weight = jnp.exp2(stats[part, :SLOTS] - tops)
        totals = totals + stats[part, SLOTS : 2 * SLOTS] * weight
        deltas = deltas + stats[part, 2 * SLOTS : 3 * SLOTS] * weight
        sums = sums + stats[part, 3 * SLOTS :]
    for part in range(4):
        merged[part, :SLOTS] = tops
        merged[part, SLOTS : 2 * SLOTS] = totals
        merged[part, 2 * SLOTS : 3 * SLOTS] = deltas
        merged[part, 3 * SLOTS :] = sums


def key_kernel(
    lists, qg, stats, shifted, grad_scores, own_tops, spare, kvout, latent, shift, delta, kacc, vacc
):
    tops = stats[0, :SLOTS]
    for part in range(1, 4):
        tops = jnp.maximum(tops, stats[part, :SLOTS])
    totals = jnp.zeros_like(tops)
    deltas = jnp.zeros_like(tops)
    sums = jnp.zeros((8, DH), jnp.float32)
    for part in range(4):
        weight = jnp.exp2(stats[part, :SLOTS] - tops)
        totals = totals + stats[part, SLOTS : 2 * SLOTS] * weight
        deltas = deltas + stats[part, 2 * SLOTS : 3 * SLOTS] * weight
        sums = sums + stats[part, 3 * SLOTS :]
    latent[...] = sums
    tops = tops + jnp.log2(totals)
    deltas = deltas / totals
    for at in range(SLOTS):
        shift[at] = tops[at : at + 1]
        delta[at] = deltas[at : at + 1]
    kacc[...] = jnp.zeros_like(kacc)
    vacc[...] = jnp.zeros_like(vacc)

    def work(pairs):
        found = []
        for head, at in pairs:
            both = lists[head, at]
            row, col = both >> 4, both & 15
            query, grad = blocks_at(qg, row, head)
            scale = jnp.exp2(own_tops[head, at] - shift[head * GB + row])
            weights = shifted[head, at] * scale
            dscore = (weights * (grad_scores[head, at] - delta[head * GB + row])).astype(jnp.bfloat16)
            kterm = dot(dscore, query, ((1,), (0,)))
            vterm = dot(weights.astype(jnp.bfloat16), grad, ((1,), (0,)))
            found.append((head * GB + col, kterm, vterm))
        for at, kterm, vterm in found:
            kacc[at] += kterm
            vacc[at] += vterm

    for_pairs(lists, work)
    for slot in range(GB):
        target = slot // 2 * 2 + ((slot & 1) ^ lists[HEADS, 2])
        for head in range(HEADS):
            first, second = head * DH, WIDE + head * DH
            kvout[target, :, first : first + DH] = kacc[head * GB + slot].astype(jnp.bfloat16)
            kvout[target, :, second : second + DH] = vacc[head * GB + slot].astype(jnp.bfloat16)


def query_kernel(lists, kv, shifted, grad_scores, own_tops, shift, delta, qout, qacc):
    qacc[...] = jnp.zeros_like(qacc)

    def work(pairs):
        found = []
        for head, at in pairs:
            both = lists[head, at]
            key, _ = blocks_at(kv, both & 15, head)
            row = head * GB + (both >> 4)
            scale = jnp.exp2(own_tops[head, at] - shift[row])
            dscore = shifted[head, at] * scale * (grad_scores[head, at] - delta[row])
            found.append((row, dot(dscore.astype(jnp.bfloat16), key, ((0,), (0,)))))
        for at, qterm in found:
            qacc[at] += qterm

    for_pairs(lists, work)
    for slot in range(GB):
        for head in range(HEADS):
            qout[slot, :, head * DH : head * DH + DH] = qacc[head * GB + slot].astype(jnp.bfloat16)


def shape(*dims, dtype=jnp.bfloat16):
    return jax.ShapeDtypeStruct(dims, dtype)


def body(queries, keys, values, out_grad, token_error, block_mask):
    qg, kv = pl.pallas_call(
        pack_kernel,
        out_shape=(shape(BLK, 2 * WIDE), shape(ROWS, 2 * WIDE)),
        in_specs=[VMEM] * 5,
        out_specs=(VMEM, VMEM),
        name="pack",
    )(queries, keys, values, out_grad, token_error)
    lists = pl.pallas_call(
        list_kernel,
        out_shape=shape(HEADS + 1, LIST, dtype=jnp.int32),
        in_specs=[SMEM, SMEM],
        out_specs=SMEM,
        compiler_params=params(4),
        name="pair_lists",
    )(block_mask, (lax.axis_index("qb") // 8).astype(jnp.int32).reshape(1))
    kv = lax.all_gather(kv, "qb", axis_index_groups=Y_PAIRS)
    kv = lax.all_gather(kv, "qb", axis_index_groups=Z_GROUPS).reshape(GB, ROWS, 2 * WIDE)
    qg = lax.all_gather(qg, "kb", axis_index_groups=Y_GROUPS)
    qg = pl.pallas_call(
        copies_kernel,
        out_shape=shape(4, 4, BLK, 2 * WIDE),
        in_specs=[VMEM],
        out_specs=pl.BlockSpec(memory_space=pl.ANY),
        scratch_shapes=[pltpu.SemaphoreType.DMA((4,))],
        compiler_params=params(4),
        name="four_copies",
    )(qg)
    spare = qg.reshape(GB, BLK, 2 * WIDE)
    qg = lax.all_to_all(qg, "kb", 0, 0, axis_index_groups=X_GROUPS).reshape(GB, BLK, 2 * WIDE)

    row_scratch = pltpu.VMEM((SLOTS, 1, DH), jnp.float32)
    block_scratch = pltpu.VMEM((SLOTS, BLK, DH), jnp.float32)
    by_pair = shape(HEADS, 2 * GB, BLK, BLK, dtype=jnp.float32)
    stats, shifted, grad_scores, tops = pl.pallas_call(
        stat_kernel,
        out_shape=(
            shape(4, STAT, DH, dtype=jnp.float32),
            by_pair,
            by_pair,
            shape(HEADS, 2 * GB, 1, DH, dtype=jnp.float32),
        ),
        in_specs=[SMEM, VMEM, VMEM],
        out_specs=(VMEM,) * 4,
        scratch_shapes=[row_scratch, row_scratch, row_scratch],
        compiler_params=params(28),
        name="row_stats",
    )(lists, qg, kv)
    stats = lax.all_to_all(stats, "kb", 0, 0, axis_index_groups=X_GROUPS)
    stats = pl.pallas_call(
        merge_kernel,
        out_shape=shape(4, STAT, DH, dtype=jnp.float32),
        in_specs=[VMEM],
        out_specs=VMEM,
        compiler_params=params(4),
        name="merge_stats",
    )(stats)
    stats = lax.all_to_all(stats, "kb", 0, 0, axis_index_groups=Y_GROUPS)
    kvpart, latent, shift, delta = pl.pallas_call(
        key_kernel,
        out_shape=(
            shape(GB, BLK, 2 * WIDE),
            shape(8, DH, dtype=jnp.float32),
            shape(SLOTS, 1, DH, dtype=jnp.float32),
            shape(SLOTS, 1, DH, dtype=jnp.float32),
        ),
        in_specs=[SMEM] + [VMEM] * 5 + [pl.BlockSpec(memory_space=pl.ANY)],
        input_output_aliases={6: 0},
        out_specs=(VMEM,) * 4,
        scratch_shapes=[block_scratch, block_scratch],
        compiler_params=params(28),
        name="key_value_grads",
    )(lists, qg, stats, shifted, grad_scores, tops, spare)
    kvpart = lax.psum_scatter(
        kvpart.reshape(8, 2 * BLK, 2 * WIDE), "qb", scatter_dimension=0, axis_index_groups=Z_GROUPS
    )
    qpart = pl.pallas_call(
        query_kernel,
        out_shape=shape(GB, BLK, WIDE),
        in_specs=[SMEM] + [VMEM] * 6,
        out_specs=VMEM,
        scratch_shapes=[block_scratch],
        compiler_params=params(28),
        name="query_grads",
    )(lists, kv, shifted, grad_scores, tops, shift, delta)
    partner = lax.ppermute(latent, "pair", [(0, 1), (1, 0)])
    own, other = latent[0, 0], partner[0, 0]
    pair_side = lax.axis_index("pair")
    winner_mean = jnp.where(pair_side == 0, own, other) / TOKENS
    loser_mean = jnp.where(pair_side == 0, other, own) / TOKENS
    keep_share = jax.nn.sigmoid(-beta_pref * (loser_mean - winner_mean))
    factor = jnp.where(pair_side == 0, 1.0 + beta_pref * keep_share, -beta_pref * keep_share)

    qpart = lax.all_to_all(qpart.reshape(4, 4, BLK, WIDE), "kb", 0, 0, axis_index_groups=X_GROUPS)
    qpart = jnp.sum(qpart.astype(jnp.float32), axis=0).astype(jnp.bfloat16)
    qpart = lax.all_to_all(qpart, "kb", 0, 0, axis_index_groups=Y_GROUPS)
    qsum = jnp.sum(qpart.astype(jnp.float32), axis=0, keepdims=True)
    query_grad = (qsum * (factor * score_scale)).astype(jnp.bfloat16)

    kvpart = kvpart.reshape(2 * BLK, 2 * WIDE)
    far = lax.ppermute(kvpart[BLK:], "qb", Y_SWAP)
    near = kvpart[:BLK]
    ksum = near[None, :, :WIDE].astype(jnp.float32) + far[None, :, :WIDE].astype(jnp.float32)
    vsum = near[None, :, WIDE:].astype(jnp.float32) + far[None, :, WIDE:].astype(jnp.float32)
    key_grad = (ksum * (factor * score_scale)).astype(jnp.bfloat16)
    value_grad = (vsum * factor).astype(jnp.bfloat16)
    return (query_grad, key_grad, value_grad)


def solution(mesh):
    return jax.shard_map(
        body,
        mesh=mesh,
        in_specs=(
            P("pair", ("qb", "kb"), None),
            P("pair", ("kb", "qb"), None),
            P("pair", ("kb", "qb"), None),
            P("pair", ("qb", "kb"), None),
            P("pair", ("qb", "kb")),
            P(None, "qb", "kb"),
        ),
        out_specs=(
            P("pair", ("qb", "kb"), None),
            P("pair", ("kb", "qb"), None),
            P("pair", ("kb", "qb"), None),
        ),
        check_vma=False,
    )
```

```python
import jax
import jax.numpy as jnp
from jax import lax
from jax.experimental import pallas as pl
from jax.experimental.pallas import tpu as pltpu
from jax.sharding import PartitionSpec as P

DH = 128
HEADS = 2
BLK = 128
GB = 16
TOKENS = 32768
WIDE = HEADS * DH
ROWS = BLK + 16
SLOTS = HEADS * GB
STAT = 3 * SLOTS + 8
LIST = 40

beta_pref = 20.0
neg_big = -1e30
score_scale = DH ** (-0.5)
log2_scale = score_scale * 1.4426950408889634

Y_GROUPS = [[x + 4 * y for y in range(4)] for x in range(4)]
X_GROUPS = [[x + 4 * y for x in range(4)] for y in range(4)]
Z_GROUPS = [[z + 8 * y for z in range(8)] for y in range(2)]
Y_PAIRS = [[z, z + 8] for z in range(8)]
Y_SWAP = [(s, s ^ 8) for s in range(16)]

VMEM = pl.BlockSpec(memory_space=pltpu.VMEM)
SMEM = pl.BlockSpec(memory_space=pltpu.SMEM)


def params(megabytes):
    return pltpu.CompilerParams(vmem_limit_bytes=megabytes * 1024 * 1024)


def dot(a, b, dims):
    return lax.dot_general(a, b, (dims, ((), ())), preferred_element_type=jnp.float32)


def pack_kernel(queries, keys, values, out_grad, token_error, qg_ref, kv_ref):
    qg_ref[:, :WIDE] = queries[0]
    qg_ref[:, WIDE:] = out_grad[0]
    total = jnp.sum(token_error[...], axis=1, keepdims=True)
    high = total.astype(jnp.bfloat16).astype(jnp.float32)
    rest = total - high
    middle = rest.astype(jnp.bfloat16).astype(jnp.float32)
    low = rest - middle
    row = lax.broadcasted_iota(jnp.int32, (16, 2 * WIDE), 0)
    sums = jnp.where(row == 0, high, jnp.where(row == 1, middle, jnp.where(row == 2, low, 0.0)))
    kv_ref[:BLK, :WIDE] = keys[0]
    kv_ref[:BLK, WIDE:] = values[0]
    kv_ref[BLK:, :] = sums.astype(jnp.bfloat16)


def copies_kernel(source, target, sems):
    copies = [pltpu.make_async_copy(source, target.at[at], sems.at[at]) for at in range(4)]
    for copy in copies:
        copy.start()
    for copy in copies:
        copy.wait()


def list_kernel(mask, side, lists):
    lists[HEADS, 2] = side[0]
    for head in range(HEADS):

        def step(row, count):
            first = ((row & 3) * 4 + (row >> 2)) * GB
            for col in range(GB):
                lists[head, count] = first + 2 * (col % 8) + col // 8
                count = jnp.minimum(count + mask[head, row, col], LIST - 1)
            return count

        lists[HEADS, head] = lax.fori_loop(0, GB, step, 0)


def for_pairs(lists, work, most=4):
    count = lists[HEADS, 0]
    whole = count // most

    def several(step, carry):
        work([(head, most * step + u) for u in range(most) for head in range(HEADS)])
        return carry

    lax.fori_loop(0, whole, several, 0)
    first, rest = whole * most, most // 2
    while rest >= 2:

        @pl.when((count & rest) != 0)
        def _(first=first, rest=rest):
            work([(head, first + u) for u in range(rest) for head in range(HEADS)])

        first, rest = first + (count & rest), rest // 2


def blocks_at(ref, slot, head):
    first, second = head * DH, WIDE + head * DH
    return ref[slot, :BLK, first : first + DH], ref[slot, :BLK, second : second + DH]


def stat_kernel(
    lists, qg, kv_from, stats, shifted, grad_scores, tops, kv_same, kv, top, total, delta, sems
):
    copies = [
        pltpu.make_async_copy(kv_from.at[pl.ds(4 * at, 4)], kv.at[pl.ds(4 * at, 4)], sems.at[at])
        for at in range(4)
    ]
    for copy in copies:
        copy.start()
    top[...] = jnp.full_like(top, neg_big)
    total[...] = jnp.zeros_like(total)
    delta[...] = jnp.zeros_like(delta)
    for copy in copies:
        copy.wait()

    def work(pairs):
        found = []
        for head, at in pairs:
            both = lists[head, at]
            row, col = both >> 4, both & 15
            query, grad = blocks_at(qg, row, head)
            key, value = blocks_at(kv, col, head)
            scores = dot(key, query, ((1,), (1,))) * log2_scale
            product = dot(value, grad, ((1,), (1,)))
            own_top = jnp.max(scores, axis=0, keepdims=True)
            weights = jnp.exp2(scores - own_top)
            shifted[head, at] = weights
            grad_scores[head, at] = product
            tops[head, at] = own_top
            own_total = jnp.sum(weights, axis=0, keepdims=True)
            own_delta = jnp.sum(weights * product, axis=0, keepdims=True)
            found.append((head * GB + row, own_top, own_total, own_delta))
        for at, own_top, own_total, own_delta in found:
            old_top = top[at]
            new_top = jnp.maximum(old_top, own_top)
            old_weight = jnp.exp2(old_top - new_top)
            own_weight = jnp.exp2(own_top - new_top)
            top[at] = new_top
            total[at] = total[at] * old_weight + own_total * own_weight
            delta[at] = delta[at] * old_weight + own_delta * own_weight

    for_pairs(lists, work, 8)
    for at in range(SLOTS):
        stats[0, at : at + 1, :] = top[at]
        stats[0, SLOTS + at : SLOTS + at + 1, :] = total[at]
        stats[0, 2 * SLOTS + at : 2 * SLOTS + at + 1, :] = delta[at]
    sums = kv[0, BLK:, :DH].astype(jnp.float32)
    for slot in range(1, GB):
        sums = sums + kv[slot, BLK:, :DH].astype(jnp.float32)
    sums = jnp.sum(sums, axis=0, keepdims=True)
    stats[0, 3 * SLOTS :, :] = jnp.broadcast_to(sums, (8, DH))
    own = stats[0]
    for part in range(1, 4):
        stats[part] = own


def merge_kernel(stats, merged):
    tops = stats[0, :SLOTS]
    for part in range(1, 4):
        tops = jnp.maximum(tops, stats[part, :SLOTS])
    totals = jnp.zeros_like(tops)
    deltas = jnp.zeros_like(tops)
    sums = jnp.zeros((8, DH), jnp.float32)
    for part in range(4):
        weight = jnp.exp2(stats[part, :SLOTS] - tops)
        totals = totals + stats[part, SLOTS : 2 * SLOTS] * weight
        deltas = deltas + stats[part, 2 * SLOTS : 3 * SLOTS] * weight
        sums = sums + stats[part, 3 * SLOTS :]
    for part in range(4):
        merged[part, :SLOTS] = tops
        merged[part, SLOTS : 2 * SLOTS] = totals
        merged[part, 2 * SLOTS : 3 * SLOTS] = deltas
        merged[part, 3 * SLOTS :] = sums


def key_kernel(
    lists, qg, stats, shifted, grad_scores, own_tops, spare, kvout, latent, shift, delta, kacc, vacc
):
    tops = stats[0, :SLOTS]
    for part in range(1, 4):
        tops = jnp.maximum(tops, stats[part, :SLOTS])
    totals = jnp.zeros_like(tops)
    deltas = jnp.zeros_like(tops)
    sums = jnp.zeros((8, DH), jnp.float32)
    for part in range(4):
        weight = jnp.exp2(stats[part, :SLOTS] - tops)
        totals = totals + stats[part, SLOTS : 2 * SLOTS] * weight
        deltas = deltas + stats[part, 2 * SLOTS : 3 * SLOTS] * weight
        sums = sums + stats[part, 3 * SLOTS :]
    latent[...] = sums
    tops = tops + jnp.log2(totals)
    deltas = deltas / totals
    for at in range(SLOTS):
        shift[at] = tops[at : at + 1]
        delta[at] = deltas[at : at + 1]
    kacc[...] = jnp.zeros_like(kacc)
    vacc[...] = jnp.zeros_like(vacc)

    def work(pairs):
        found = []
        for head, at in pairs:
            both = lists[head, at]
            row, col = both >> 4, both & 15
            query, grad = blocks_at(qg, row, head)
            scale = jnp.exp2(own_tops[head, at] - shift[head * GB + row])
            weights = shifted[head, at] * scale
            dscore = (weights * (grad_scores[head, at] - delta[head * GB + row])).astype(jnp.bfloat16)
            kterm = dot(dscore, query, ((1,), (0,)))
            vterm = dot(weights.astype(jnp.bfloat16), grad, ((1,), (0,)))
            found.append((head * GB + col, kterm, vterm))
        for at, kterm, vterm in found:
            kacc[at] += kterm
            vacc[at] += vterm

    for_pairs(lists, work)
    for slot in range(GB):
        target = slot // 2 * 2 + ((slot & 1) ^ lists[HEADS, 2])
        for head in range(HEADS):
            first, second = head * DH, WIDE + head * DH
            kvout[target, :, first : first + DH] = kacc[head * GB + slot].astype(jnp.bfloat16)
            kvout[target, :, second : second + DH] = vacc[head * GB + slot].astype(jnp.bfloat16)


def query_kernel(lists, kv, shifted, grad_scores, own_tops, shift, delta, qout, qacc):
    qacc[...] = jnp.zeros_like(qacc)

    def work(pairs):
        found = []
        for head, at in pairs:
            both = lists[head, at]
            key, _ = blocks_at(kv, both & 15, head)
            row = head * GB + (both >> 4)
            scale = jnp.exp2(own_tops[head, at] - shift[row])
            dscore = shifted[head, at] * scale * (grad_scores[head, at] - delta[row])
            found.append((row, dot(dscore.astype(jnp.bfloat16), key, ((0,), (0,)))))
        for at, qterm in found:
            qacc[at] += qterm

    for_pairs(lists, work)
    for slot in range(GB):
        for head in range(HEADS):
            qout[slot, :, head * DH : head * DH + DH] = qacc[head * GB + slot].astype(jnp.bfloat16)


def shape(*dims, dtype=jnp.bfloat16):
    return jax.ShapeDtypeStruct(dims, dtype)


def body(queries, keys, values, out_grad, token_error, block_mask):
    qg, kv = pl.pallas_call(
        pack_kernel,
        out_shape=(shape(BLK, 2 * WIDE), shape(ROWS, 2 * WIDE)),
        in_specs=[VMEM] * 5,
        out_specs=(VMEM, VMEM),
        name="pack",
    )(queries, keys, values, out_grad, token_error)
    lists = pl.pallas_call(
        list_kernel,
        out_shape=shape(HEADS + 1, LIST, dtype=jnp.int32),
        in_specs=[SMEM, SMEM],
        out_specs=SMEM,
        compiler_params=params(4),
        name="pair_lists",
    )(block_mask, (lax.axis_index("qb") // 8).astype(jnp.int32).reshape(1))
    kv = lax.all_gather(kv, "qb", axis_index_groups=Y_PAIRS)
    kv = lax.all_gather(kv, "qb", axis_index_groups=Z_GROUPS).reshape(GB, ROWS, 2 * WIDE)
    qg = lax.all_gather(qg, "kb", axis_index_groups=Y_GROUPS)
    qg = pl.pallas_call(
        copies_kernel,
        out_shape=shape(4, 4, BLK, 2 * WIDE),
        in_specs=[VMEM],
        out_specs=pl.BlockSpec(memory_space=pl.ANY),
        scratch_shapes=[pltpu.SemaphoreType.DMA((4,))],
        compiler_params=params(4),
        name="four_copies",
    )(qg)
    spare = qg.reshape(GB, BLK, 2 * WIDE)
    qg = lax.all_to_all(qg, "kb", 0, 0, axis_index_groups=X_GROUPS).reshape(GB, BLK, 2 * WIDE)

    row_scratch = pltpu.VMEM((SLOTS, 1, DH), jnp.float32)
    block_scratch = pltpu.VMEM((SLOTS, BLK, DH), jnp.float32)
    by_pair = shape(HEADS, 2 * GB, BLK, BLK, dtype=jnp.float32)
    stats, shifted, grad_scores, tops, kv = pl.pallas_call(
        stat_kernel,
        out_shape=(
            shape(4, STAT, DH, dtype=jnp.float32),
            by_pair,
            by_pair,
            shape(HEADS, 2 * GB, 1, DH, dtype=jnp.float32),
            shape(GB, ROWS, 2 * WIDE),
        ),
        in_specs=[SMEM, VMEM, pl.BlockSpec(memory_space=pl.ANY)],
        out_specs=(VMEM,) * 4 + (pl.BlockSpec(memory_space=pl.ANY),),
        input_output_aliases={2: 4},
        scratch_shapes=[
            pltpu.VMEM((GB, ROWS, 2 * WIDE), jnp.bfloat16),
            row_scratch,
            row_scratch,
            row_scratch,
            pltpu.SemaphoreType.DMA((4,)),
        ],
        compiler_params=params(28),
        name="row_stats",
    )(lists, qg, kv)
    stats = lax.all_to_all(stats, "kb", 0, 0, axis_index_groups=X_GROUPS)
    stats = pl.pallas_call(
        merge_kernel,
        out_shape=shape(4, STAT, DH, dtype=jnp.float32),
        in_specs=[VMEM],
        out_specs=VMEM,
        compiler_params=params(4),
        name="merge_stats",
    )(stats)
    stats = lax.all_to_all(stats, "kb", 0, 0, axis_index_groups=Y_GROUPS)
    kvpart, latent, shift, delta = pl.pallas_call(
        key_kernel,
        out_shape=(
            shape(GB, BLK, 2 * WIDE),
            shape(8, DH, dtype=jnp.float32),
            shape(SLOTS, 1, DH, dtype=jnp.float32),
            shape(SLOTS, 1, DH, dtype=jnp.float32),
        ),
        in_specs=[SMEM] + [VMEM] * 5 + [pl.BlockSpec(memory_space=pl.ANY)],
        input_output_aliases={6: 0},
        out_specs=(VMEM,) * 4,
        scratch_shapes=[block_scratch, block_scratch],
        compiler_params=params(28),
        name="key_value_grads",
    )(lists, qg, stats, shifted, grad_scores, tops, spare)
    kvpart = lax.psum_scatter(
        kvpart.reshape(8, 2 * BLK, 2 * WIDE), "qb", scatter_dimension=0, axis_index_groups=Z_GROUPS
    )
    qpart = pl.pallas_call(
        query_kernel,
        out_shape=shape(GB, BLK, WIDE),
        in_specs=[SMEM] + [VMEM] * 6,
        out_specs=VMEM,
        scratch_shapes=[block_scratch],
        compiler_params=params(28),
        name="query_grads",
    )(lists, kv, shifted, grad_scores, tops, shift, delta)
    partner = lax.ppermute(latent, "pair", [(0, 1), (1, 0)])
    own, other = latent[0, 0], partner[0, 0]
    pair_side = lax.axis_index("pair")
    winner_mean = jnp.where(pair_side == 0, own, other) / TOKENS
    loser_mean = jnp.where(pair_side == 0, other, own) / TOKENS
    keep_share = jax.nn.sigmoid(-beta_pref * (loser_mean - winner_mean))
    factor = jnp.where(pair_side == 0, 1.0 + beta_pref * keep_share, -beta_pref * keep_share)

    qpart = lax.all_to_all(qpart.reshape(4, 4, BLK, WIDE), "kb", 0, 0, axis_index_groups=X_GROUPS)
    qpart = jnp.sum(qpart.astype(jnp.float32), axis=0).astype(jnp.bfloat16)
    qpart = lax.all_to_all(qpart, "kb", 0, 0, axis_index_groups=Y_GROUPS)
    qsum = jnp.sum(qpart.astype(jnp.float32), axis=0, keepdims=True)
    query_grad = (qsum * (factor * score_scale)).astype(jnp.bfloat16)

    kvpart = kvpart.reshape(2 * BLK, 2 * WIDE)
    far = lax.ppermute(kvpart[BLK:], "qb", Y_SWAP)
    near = kvpart[:BLK]
    ksum = near[None, :, :WIDE].astype(jnp.float32) + far[None, :, :WIDE].astype(jnp.float32)
    vsum = near[None, :, WIDE:].astype(jnp.float32) + far[None, :, WIDE:].astype(jnp.float32)
    key_grad = (ksum * (factor * score_scale)).astype(jnp.bfloat16)
    value_grad = (vsum * factor).astype(jnp.bfloat16)
    return (query_grad, key_grad, value_grad)


def solution(mesh):
    return jax.shard_map(
        body,
        mesh=mesh,
        in_specs=(
            P("pair", ("qb", "kb"), None),
            P("pair", ("kb", "qb"), None),
            P("pair", ("kb", "qb"), None),
            P("pair", ("qb", "kb"), None),
            P("pair", ("qb", "kb")),
            P(None, "qb", "kb"),
        ),
        out_specs=(
            P("pair", ("qb", "kb"), None),
            P("pair", ("kb", "qb"), None),
            P("pair", ("kb", "qb"), None),
        ),
        check_vma=False,
    )
```

```python
import jax
import jax.numpy as jnp
from jax import lax
from jax.experimental import pallas as pl
from jax.experimental.pallas import tpu as pltpu
from jax.sharding import PartitionSpec as P

DH = 128
HEADS = 2
BLK = 128
GB = 16
TOKENS = 32768
WIDE = HEADS * DH
ROWS = BLK + 16
SLOTS = HEADS * GB
STAT = 3 * SLOTS + 8
LIST = 40

beta_pref = 20.0
neg_big = -1e30
score_scale = DH ** (-0.5)
log2_scale = score_scale * 1.4426950408889634

Y_GROUPS = [[x + 4 * y for y in range(4)] for x in range(4)]
X_GROUPS = [[x + 4 * y for x in range(4)] for y in range(4)]
Z_GROUPS = [[z + 8 * y for z in range(8)] for y in range(2)]
Y_PAIRS = [[z, z + 8] for z in range(8)]
Y_SWAP = [(s, s ^ 8) for s in range(16)]

VMEM = pl.BlockSpec(memory_space=pltpu.VMEM)
SMEM = pl.BlockSpec(memory_space=pltpu.SMEM)


def params(megabytes):
    return pltpu.CompilerParams(vmem_limit_bytes=megabytes * 1024 * 1024)


def dot(a, b, dims):
    return lax.dot_general(a, b, (dims, ((), ())), preferred_element_type=jnp.float32)


def pack_kernel(queries, keys, values, out_grad, token_error, qg_ref, kv_ref):
    qg_ref[:, :WIDE] = queries[0]
    qg_ref[:, WIDE:] = out_grad[0]
    total = jnp.sum(token_error[...], axis=1, keepdims=True)
    high = total.astype(jnp.bfloat16).astype(jnp.float32)
    rest = total - high
    middle = rest.astype(jnp.bfloat16).astype(jnp.float32)
    low = rest - middle
    row = lax.broadcasted_iota(jnp.int32, (16, 2 * WIDE), 0)
    sums = jnp.where(row == 0, high, jnp.where(row == 1, middle, jnp.where(row == 2, low, 0.0)))
    kv_ref[:BLK, :WIDE] = keys[0]
    kv_ref[:BLK, WIDE:] = values[0]
    kv_ref[BLK:, :] = sums.astype(jnp.bfloat16)


def copies_kernel(source, target, sems):
    copies = [pltpu.make_async_copy(source, target.at[at], sems.at[at]) for at in range(4)]
    for copy in copies:
        copy.start()
    for copy in copies:
        copy.wait()


def list_kernel(mask, side, lists):
    lists[HEADS, 2] = side[0]
    for head in range(HEADS):

        def step(row, count):
            first = ((row & 3) * 4 + (row >> 2)) * GB
            for col in range(GB):
                lists[head, count] = first + 2 * (col % 8) + col // 8
                count = jnp.minimum(count + mask[head, row, col], LIST - 1)
            return count

        lists[HEADS, head] = lax.fori_loop(0, GB, step, 0)


def for_pairs(lists, work, most=4):
    count = lists[HEADS, 0]
    whole = count // most

    def several(step, carry):
        work([(head, most * step + u) for u in range(most) for head in range(HEADS)])
        return carry

    lax.fori_loop(0, whole, several, 0)
    first, rest = whole * most, most // 2
    while rest >= 2:

        @pl.when((count & rest) != 0)
        def _(first=first, rest=rest):
            work([(head, first + u) for u in range(rest) for head in range(HEADS)])

        first, rest = first + (count & rest), rest // 2


def blocks_at(ref, slot, head):
    first, second = head * DH, WIDE + head * DH
    return ref[slot, :BLK, first : first + DH], ref[slot, :BLK, second : second + DH]


def stat_kernel(lists, qg, kv, stats, shifted, grad_scores, tops, top, total, delta):
    top[...] = jnp.full_like(top, neg_big)
    total[...] = jnp.zeros_like(total)
    delta[...] = jnp.zeros_like(delta)

    def work(pairs):
        found = []
        for head, at in pairs:
            both = lists[head, at]
            row, col = both >> 4, both & 15
            query, grad = blocks_at(qg, row, head)
            key, value = blocks_at(kv, col, head)
            scores = dot(key, query, ((1,), (1,))) * log2_scale
            product = dot(value, grad, ((1,), (1,)))
            own_top = jnp.max(scores, axis=0, keepdims=True)
            weights = jnp.exp2(scores - own_top)
            shifted[head, at] = weights
            grad_scores[head, at] = product
            tops[head, at] = own_top
            own_total = jnp.sum(weights, axis=0, keepdims=True)
            own_delta = jnp.sum(weights * product, axis=0, keepdims=True)
            found.append((head * GB + row, own_top, own_total, own_delta))
        for at, own_top, own_total, own_delta in found:
            old_top = top[at]
            new_top = jnp.maximum(old_top, own_top)
            old_weight = jnp.exp2(old_top - new_top)
            own_weight = jnp.exp2(own_top - new_top)
            top[at] = new_top
            total[at] = total[at] * old_weight + own_total * own_weight
            delta[at] = delta[at] * old_weight + own_delta * own_weight

    for_pairs(lists, work, 8)
    for at in range(SLOTS):
        stats[0, at : at + 1, :] = top[at]
        stats[0, SLOTS + at : SLOTS + at + 1, :] = total[at]
        stats[0, 2 * SLOTS + at : 2 * SLOTS + at + 1, :] = delta[at]
    sums = kv[0, BLK:, :DH].astype(jnp.float32)
    for slot in range(1, GB):
        sums = sums + kv[slot, BLK:, :DH].astype(jnp.float32)
    sums = jnp.sum(sums, axis=0, keepdims=True)
    stats[0, 3 * SLOTS :, :] = jnp.broadcast_to(sums, (8, DH))
    own = stats[0]
    for part in range(1, 4):
        stats[part] = own


def merge_kernel(stats, merged):
    tops = stats[0, :SLOTS]
    for part in range(1, 4):
        tops = jnp.maximum(tops, stats[part, :SLOTS])
    totals = jnp.zeros_like(tops)
    deltas = jnp.zeros_like(tops)
    sums = jnp.zeros((8, DH), jnp.float32)
    for part in range(4):
        weight = jnp.exp2(stats[part, :SLOTS] - tops)
        totals = totals + stats[part, SLOTS : 2 * SLOTS] * weight
        deltas = deltas + stats[part, 2 * SLOTS : 3 * SLOTS] * weight
        sums = sums + stats[part, 3 * SLOTS :]
    for part in range(4):
        merged[part, :SLOTS] = tops
        merged[part, SLOTS : 2 * SLOTS] = totals
        merged[part, 2 * SLOTS : 3 * SLOTS] = deltas
        merged[part, 3 * SLOTS :] = sums


def key_kernel(
    lists, qg, stats, shifted, grad_scores, own_tops, spare, kvout, latent, shift, delta, kacc, vacc
):
    tops = stats[0, :SLOTS]
    for part in range(1, 4):
        tops = jnp.maximum(tops, stats[part, :SLOTS])
    totals = jnp.zeros_like(tops)
    deltas = jnp.zeros_like(tops)
    sums = jnp.zeros((8, DH), jnp.float32)
    for part in range(4):
        weight = jnp.exp2(stats[part, :SLOTS] - tops)
        totals = totals + stats[part, SLOTS : 2 * SLOTS] * weight
        deltas = deltas + stats[part, 2 * SLOTS : 3 * SLOTS] * weight
        sums = sums + stats[part, 3 * SLOTS :]
    latent[...] = sums
    tops = tops + jnp.log2(totals)
    deltas = deltas / totals
    for at in range(SLOTS):
        shift[at] = tops[at : at + 1]
        delta[at] = deltas[at : at + 1]
    kacc[...] = jnp.zeros_like(kacc)
    vacc[...] = jnp.zeros_like(vacc)

    def work(pairs):
        found = []
        for head, at in pairs:
            both = lists[head, at]
            row, col = both >> 4, both & 15
            query, grad = blocks_at(qg, row, head)
            scale = jnp.exp2(own_tops[head, at] - shift[head * GB + row])
            weights = shifted[head, at] * scale
            dscore = (weights * (grad_scores[head, at] - delta[head * GB + row])).astype(jnp.bfloat16)
            kterm = dot(dscore, query, ((1,), (0,)))
            vterm = dot(weights.astype(jnp.bfloat16), grad, ((1,), (0,)))
            found.append((head * GB + col, kterm, vterm))
        for at, kterm, vterm in found:
            kacc[at] += kterm
            vacc[at] += vterm

    for_pairs(lists, work, 8)
    for slot in range(GB):
        target = slot // 2 * 2 + ((slot & 1) ^ lists[HEADS, 2])
        for head in range(HEADS):
            first, second = head * DH, WIDE + head * DH
            kvout[target, :, first : first + DH] = kacc[head * GB + slot].astype(jnp.bfloat16)
            kvout[target, :, second : second + DH] = vacc[head * GB + slot].astype(jnp.bfloat16)


def query_kernel(lists, kv, shifted, grad_scores, own_tops, shift, delta, qout, qacc):
    qacc[...] = jnp.zeros_like(qacc)

    def work(pairs):
        found = []
        for head, at in pairs:
            both = lists[head, at]
            key, _ = blocks_at(kv, both & 15, head)
            row = head * GB + (both >> 4)
            scale = jnp.exp2(own_tops[head, at] - shift[row])
            dscore = shifted[head, at] * scale * (grad_scores[head, at] - delta[row])
            found.append((row, dot(dscore.astype(jnp.bfloat16), key, ((0,), (0,)))))
        for at, qterm in found:
            qacc[at] += qterm

    for_pairs(lists, work)
    for slot in range(GB):
        for head in range(HEADS):
            qout[slot, :, head * DH : head * DH + DH] = qacc[head * GB + slot].astype(jnp.bfloat16)


def shape(*dims, dtype=jnp.bfloat16):
    return jax.ShapeDtypeStruct(dims, dtype)


def body(queries, keys, values, out_grad, token_error, block_mask):
    qg, kv = pl.pallas_call(
        pack_kernel,
        out_shape=(shape(BLK, 2 * WIDE), shape(ROWS, 2 * WIDE)),
        in_specs=[VMEM] * 5,
        out_specs=(VMEM, VMEM),
        name="pack",
    )(queries, keys, values, out_grad, token_error)
    lists = pl.pallas_call(
        list_kernel,
        out_shape=shape(HEADS + 1, LIST, dtype=jnp.int32),
        in_specs=[SMEM, SMEM],
        out_specs=SMEM,
        compiler_params=params(4),
        name="pair_lists",
    )(block_mask, (lax.axis_index("qb") // 8).astype(jnp.int32).reshape(1))
    kv = lax.all_gather(kv, "qb", axis_index_groups=Y_PAIRS)
    kv = lax.all_gather(kv, "qb", axis_index_groups=Z_GROUPS).reshape(GB, ROWS, 2 * WIDE)
    qg = lax.all_gather(qg, "kb", axis_index_groups=Y_GROUPS)
    qg = pl.pallas_call(
        copies_kernel,
        out_shape=shape(4, 4, BLK, 2 * WIDE),
        in_specs=[VMEM],
        out_specs=pl.BlockSpec(memory_space=pl.ANY),
        scratch_shapes=[pltpu.SemaphoreType.DMA((4,))],
        compiler_params=params(4),
        name="four_copies",
    )(qg)
    spare = qg.reshape(GB, BLK, 2 * WIDE)
    qg = lax.all_to_all(qg, "kb", 0, 0, axis_index_groups=X_GROUPS).reshape(GB, BLK, 2 * WIDE)

    row_scratch = pltpu.VMEM((SLOTS, 1, DH), jnp.float32)
    block_scratch = pltpu.VMEM((SLOTS, BLK, DH), jnp.float32)
    by_pair = shape(HEADS, 2 * GB, BLK, BLK, dtype=jnp.float32)
    stats, shifted, grad_scores, tops = pl.pallas_call(
        stat_kernel,
        out_shape=(
            shape(4, STAT, DH, dtype=jnp.float32),
            by_pair,
            by_pair,
            shape(HEADS, 2 * GB, 1, DH, dtype=jnp.float32),
        ),
        in_specs=[SMEM, VMEM, VMEM],
        out_specs=(VMEM,) * 4,
        scratch_shapes=[row_scratch, row_scratch, row_scratch],
        compiler_params=params(28),
        name="row_stats",
    )(lists, qg, kv)
    stats = lax.all_to_all(stats, "kb", 0, 0, axis_index_groups=X_GROUPS)
    stats = pl.pallas_call(
        merge_kernel,
        out_shape=shape(4, STAT, DH, dtype=jnp.float32),
        in_specs=[VMEM],
        out_specs=VMEM,
        compiler_params=params(4),
        name="merge_stats",
    )(stats)
    stats = lax.all_to_all(stats, "kb", 0, 0, axis_index_groups=Y_GROUPS)
    kvpart, latent, shift, delta = pl.pallas_call(
        key_kernel,
        out_shape=(
            shape(GB, BLK, 2 * WIDE),
            shape(8, DH, dtype=jnp.float32),
            shape(SLOTS, 1, DH, dtype=jnp.float32),
            shape(SLOTS, 1, DH, dtype=jnp.float32),
        ),
        in_specs=[SMEM] + [VMEM] * 5 + [pl.BlockSpec(memory_space=pl.ANY)],
        input_output_aliases={6: 0},
        out_specs=(VMEM,) * 4,
        scratch_shapes=[block_scratch, block_scratch],
        compiler_params=params(28),
        name="key_value_grads",
    )(lists, qg, stats, shifted, grad_scores, tops, spare)
    kvpart = lax.psum_scatter(
        kvpart.reshape(8, 2 * BLK, 2 * WIDE), "qb", scatter_dimension=0, axis_index_groups=Z_GROUPS
    )
    qpart = pl.pallas_call(
        query_kernel,
        out_shape=shape(GB, BLK, WIDE),
        in_specs=[SMEM] + [VMEM] * 6,
        out_specs=VMEM,
        scratch_shapes=[block_scratch],
        compiler_params=params(28),
        name="query_grads",
    )(lists, kv, shifted, grad_scores, tops, shift, delta)
    partner = lax.ppermute(latent, "pair", [(0, 1), (1, 0)])
    own, other = latent[0, 0], partner[0, 0]
    pair_side = lax.axis_index("pair")
    winner_mean = jnp.where(pair_side == 0, own, other) / TOKENS
    loser_mean = jnp.where(pair_side == 0, other, own) / TOKENS
    keep_share = jax.nn.sigmoid(-beta_pref * (loser_mean - winner_mean))
    factor = jnp.where(pair_side == 0, 1.0 + beta_pref * keep_share, -beta_pref * keep_share)

    qpart = lax.all_to_all(qpart.reshape(4, 4, BLK, WIDE), "kb", 0, 0, axis_index_groups=X_GROUPS)
    qpart = jnp.sum(qpart.astype(jnp.float32), axis=0).astype(jnp.bfloat16)
    qpart = lax.all_to_all(qpart, "kb", 0, 0, axis_index_groups=Y_GROUPS)
    qsum = jnp.sum(qpart.astype(jnp.float32), axis=0, keepdims=True)
    query_grad = (qsum * (factor * score_scale)).astype(jnp.bfloat16)

    kvpart = kvpart.reshape(2 * BLK, 2 * WIDE)
    far = lax.ppermute(kvpart[BLK:], "qb", Y_SWAP)
    near = kvpart[:BLK]
    ksum = near[None, :, :WIDE].astype(jnp.float32) + far[None, :, :WIDE].astype(jnp.float32)
    vsum = near[None, :, WIDE:].astype(jnp.float32) + far[None, :, WIDE:].astype(jnp.float32)
    key_grad = (ksum * (factor * score_scale)).astype(jnp.bfloat16)
    value_grad = (vsum * factor).astype(jnp.bfloat16)
    return (query_grad, key_grad, value_grad)


def solution(mesh):
    return jax.shard_map(
        body,
        mesh=mesh,
        in_specs=(
            P("pair", ("qb", "kb"), None),
            P("pair", ("kb", "qb"), None),
            P("pair", ("kb", "qb"), None),
            P("pair", ("qb", "kb"), None),
            P("pair", ("qb", "kb")),
            P(None, "qb", "kb"),
        ),
        out_specs=(
            P("pair", ("qb", "kb"), None),
            P("pair", ("kb", "qb"), None),
            P("pair", ("kb", "qb"), None),
        ),
        check_vma=False,
    )
```
